256 devices in a mesh: query: 32 (over x, z_hi, y), entity: 8 (over z_lo, core).
Axes of the slice: x: 4, y: 4, z: 8 (z_hi: 2, z_lo: 4; z = z_hi * 4 + z_lo), core: 2. Of those that a mesh axis runs over, the one named last changes fastest.
Arguments:
- anchor_ids: int32 [16384], P('query'), may hold values from 0 to 32767
- relation_ids: int32 [16384], P('query'), may hold values from 0 to 4130
- side_flags: int32 [16384], P('query'), may hold values from 0 to 1
- teacher_entities: bfloat16 [32768, 1000], P(('entity', 'query')), may hold values from -1.2 to 1.2, as said below
- student_entities: bfloat16 [32768, 128], P(('entity', 'query')), may hold values from -2.1 to 2.1, as said below
- teacher_relations: bfloat16 [4131, 1000], replicated, may hold values from -9 to 33, as said below
- student_relations: bfloat16 [4131, 128], replicated, may hold values from -9 to 63.6875, as said below
Outputs:
- divergence: float32 [16384], P('query')
- entity_grad: float32 [32768, 128], P(('entity', 'query'))
- query_grad: float32 [16384, 128], P('query')
The draws below stay inside these ranges and needn't reach their ends.
Inputs may be any that keep to these rules, and one draw needn't show every extreme that they name: `teacher_entities`: Real-valued embeddings. `student_entities`: Real-valued embeddings. `teacher_relations`: Real-valued embeddings. `student_relations`: Real-valued embeddings.
All inputs are finite; a program needn't handle non-finite values.
Results may differ from the reference program's by a relative error of at most 0.013.
Values may be sent and summed in bfloat16 or wider, within the bound.
A program may use at most 128 MiB of HBM per device.

```python
import math
import jax
import jax.numpy as jnp
import numpy as np
from jax import lax

TW = 1000
SW = 128
REL = 4131
ENTITIES = 32768
QUERIES = 16384


def entity_table(key, width, sigma):
    first, second = jax.random.split(key, 2)
    third = jax.random.fold_in(key, 5)
    base = jax.random.truncated_normal(first, -4.0, 4.0, (ENTITIES, width), jnp.float32)
    scale = jnp.exp(jax.random.uniform(second, (ENTITIES, 1), jnp.float32, math.log(0.5), math.log(2.0)))
    table = base * scale * sigma
    fresh = jax.random.truncated_normal(third, -4.0, 4.0, (ENTITIES, width), jnp.float32) * sigma
    pairs = table.reshape(ENTITIES // 2, 2, width)
    noise = fresh.reshape(ENTITIES // 2, 2, width)
    partner = 0.985 * pairs[:, 0, :] + 0.3 * noise[:, 1, :]
    joined = jnp.stack([pairs[:, 0, :], partner], axis=1)
    return joined.reshape(ENTITIES, width)


def relation_table(key, width, per_entry, chance):
    half = width // 2
    first, second, third = jax.random.split(key, 3)
    base = jax.random.truncated_normal(first, -6.0, 6.0, (REL, width), jnp.float32) * 1.5
    strong = jax.random.bernoulli(second, chance, (REL, 1)).astype(jnp.float32)
    strength = jax.random.uniform(third, (REL, 1), jnp.float32, 1.0, 3.0)
    offset = strong * strength * (150.0 / (half * per_entry))
    columns = (jnp.arange(width)[None, :] < half).astype(jnp.float32)
    return base + offset * columns


def draw_teacher_entities(key, part):
    return entity_table(jax.random.fold_in(key, 11), TW, 0.12).astype(jnp.bfloat16)


def draw_student_entities(key, part):
    return entity_table(jax.random.fold_in(key, 23), SW, 0.22).astype(jnp.bfloat16)


def draw_teacher_relations(key, part):
    key = jax.random.fold_in(key, 37)
    chance = 0.0
    return relation_table(key, TW, 0.039, chance).astype(jnp.bfloat16)


def draw_student_relations(key, part):
    key = jax.random.fold_in(key, 41)
    chance = 0.0
    return relation_table(key, SW, 0.131, chance).astype(jnp.bfloat16)


def set_ends(drawn, rng, least, top_value):
    longest = drawn.shape.index(max(drawn.shape))
    spots = []
    for shift in (0, 1):
        where = [jax.random.randint(jax.random.fold_in(rng, axis), (), 0, length) for axis, length in enumerate(drawn.shape)]
        where[longest] = (where[longest] + shift) % drawn.shape[longest]
        spots.append(tuple(where))
    return drawn.at[spots[0]].set(least).at[spots[1]].set(top_value)


def rank_bounds(count, slope):
    portions = [(1 << 20) // math.isqrt(rank ** slope) + 1 for rank in range(1, count + 1)]
    spread = 1 + sum(portions) // (1 << 30)
    return np.cumsum(np.array([max(1, weight // spread) for weight in portions]))


def ranked_ids(rng, shape, number_of, skew):
    table = rank_bounds(number_of, skew)
    lot = jax.random.randint(jax.random.fold_in(rng, 1), shape, 0, int(table[number_of - 1]))
    rank = jnp.searchsorted(jnp.asarray(table, jnp.int32), lot, side="right")
    return jax.random.permutation(jax.random.fold_in(rng, 2), number_of)[rank].astype(jnp.int32)


def setup_inputs(seed: int = 0) -> dict:
    key_list = jax.random.split(jax.random.key(seed), 8)
    anchor_ids = set_ends(jax.random.randint(key_list[0], (QUERIES,), 0, ENTITIES), jax.random.fold_in(key_list[0], 1), 0, ENTITIES - 1).astype(jnp.int32)
    relation_ids = set_ends(ranked_ids(key_list[1], (QUERIES,), REL, 2), jax.random.fold_in(key_list[1], 3), 0, REL - 1).astype(jnp.int32)
    side_flags = set_ends(jax.random.randint(key_list[2], (QUERIES,), 0, 2), jax.random.fold_in(key_list[2], 1), 0, 1).astype(jnp.int32)
    teacher_entities = draw_teacher_entities(jax.random.fold_in(key_list[7], 71), 0)
    student_entities = draw_student_entities(jax.random.fold_in(key_list[7], 71), 0)
    teacher_relations = draw_teacher_relations(jax.random.fold_in(key_list[7], 71), 0)
    student_relations = draw_student_relations(jax.random.fold_in(key_list[7], 71), 0)
    return dict(anchor_ids=anchor_ids, relation_ids=relation_ids, side_flags=side_flags, teacher_entities=teacher_entities, student_entities=student_entities, teacher_relations=teacher_relations, student_relations=student_relations)


def query_vectors(anchor, relation, flags):
    half = anchor.shape[1] // 2
    sign = (2 * flags - 1).astype(jnp.float32)[:, None]
    a_re = anchor[:, :half]
    a_im = anchor[:, half:]
    r_re = relation[:, :half]
    r_im = relation[:, half:]
    real = a_re * r_re - sign * a_im * r_im
    imag = a_im * r_re + sign * a_re * r_im
    return jnp.concatenate([real, imag], axis=1).astype(jnp.bfloat16)


def reference(anchor_ids, relation_ids, side_flags, teacher_entities, student_entities, teacher_relations, student_relations):
    query_teacher = query_vectors(teacher_entities[anchor_ids].astype(jnp.float32), teacher_relations[relation_ids].astype(jnp.float32), side_flags)
    query_student = query_vectors(student_entities[anchor_ids].astype(jnp.float32), student_relations[relation_ids].astype(jnp.float32), side_flags)
    width = min(256, QUERIES)
    count = QUERIES // width
    teacher_blocks = query_teacher.reshape(count, width, TW)
    student_blocks = query_student.reshape(count, width, SW)

    def step(grad_total, items):
        q_teacher, q_student = items
        t = jnp.dot(q_teacher, teacher_entities.T, preferred_element_type=jnp.float32)
        s = jnp.dot(q_student, student_entities.T, preferred_element_type=jnp.float32)
        top_t = jnp.max(t, axis=1)
        top_s = jnp.max(s, axis=1)
        total_t = jnp.sum(jnp.exp(t - top_t[:, None]), axis=1)
        total_s = jnp.sum(jnp.exp(s - top_s[:, None]), axis=1)
        prob_t = jnp.exp(t - top_t[:, None]) / total_t[:, None]
        prob_s = jnp.exp(s - top_s[:, None]) / total_s[:, None]
        diverge = jnp.sum(prob_t * (t - s), axis=1) - top_t - jnp.log(total_t) + top_s + jnp.log(total_s)
        weights = (prob_s - prob_t).astype(jnp.bfloat16)
        grad_total = grad_total + jnp.dot(weights.T, q_student, preferred_element_type=jnp.float32)
        q_grad = jnp.dot(weights, student_entities, preferred_element_type=jnp.float32)
        return grad_total, (diverge, q_grad)

    start = jnp.zeros((ENTITIES, SW), jnp.float32)
    entity_grad, (diverge, q_grad) = lax.scan(step, start, (teacher_blocks, student_blocks))
    return diverge.reshape(QUERIES), entity_grad, q_grad.reshape(QUERIES, SW)
```

```python
import jax
import jax.numpy as jnp
from jax import lax
from jax.experimental import pallas as pl
from jax.experimental.pallas import tpu as pltpu
from jax.sharding import PartitionSpec as P

MESH = pl.DeviceIdType.MESH
BF = jnp.bfloat16
F32 = jnp.float32
GROUP = 512
ROWS = 2 * GROUP
ENT = 128
HALF = 500
PAD = 512
BLK = ENT + 2 * PAD
CUT = BLK // 2
REL = 4131
RELA = 4096
SHARD = 64
BIT = 32


def slot(sd, fd):
    return sd * 4 + fd


def dot_nn(a, b):
    return lax.dot_general(a, b, (((1,), (0,)), ((), ())), preferred_element_type=F32)


def dot_nt(a, b):
    return lax.dot_general(a, b, (((1,), (1,)), ((), ())), preferred_element_type=F32)


def kernel(
    meta,
    ent_t,
    ent_s,
    rel_t,
    rel_s,
    div_out,
    eg_out,
    qg_out,
    slab,
    rtv,
    rsv,
    wide,
    mids,
    mrow,
    mcol,
    idb,
    abuf,
    dbuf,
    sumb,
    rbuf,
    racc,
    rsacc,
    qbuf,
    tbuf,
    sbuf,
    mxt,
    mxs,
    zt_acc,
    w_acc,
    zs_acc,
    own_st,
    mate_st,
    st,
    fin,
    ftb,
    fsb,
    qst,
    eg_own,
    eg_s,
    eg_sr,
    eg_f,
    eg_fr,
    qg,
    qgb,
    qgd,
    qgsum,
    qgz,
    qgr,
    qgo,
    loc_sem,
    send_sem,
    recv_sem,
):
    q = lax.axis_index("query")
    e = lax.axis_index("entity")
    x, zh, y = lax.div(q, 8), lax.rem(lax.div(q, 4), 2), lax.rem(q, 4)
    zl, core = lax.div(e, 2), lax.rem(e, 2)
    z = zh * 4 + zl
    first = x + core * (y - x)
    second = y + core * (x - y)

    def dev(fd, sd):
        a, b = lax.rem(first + fd, 4), lax.rem(second + sd, 4)
        return (a + core * (b - a)) * 8 + zh * 4 + b + core * (a - b)

    def zdev(d):
        zz = lax.rem(z + d, 8)
        return (x * 8 + lax.div(zz, 4) * 4 + y, lax.rem(zz, 4) * 2 + core)

    mate = (q, zl * 2 + 1 - core)

    rt_copy = pltpu.make_async_copy(rel_t, rtv, loc_sem.at[0])
    rt_copy.start()
    rs_copy = pltpu.make_async_copy(rel_s, rsv, loc_sem.at[1])
    rs_copy.start()

    barrier = pltpu.get_barrier_semaphore()
    peers = [(dev(d, 0), e) for d in (1, 2, 3)]
    peers += [(dev(0, d), e) for d in (1, 2, 3)]
    peers += [zdev(d) for d in range(1, 8)]
    peers += [mate]
    for peer in peers:
        pl.semaphore_signal(barrier, inc=1, device_id=peer, device_id_type=MESH)

    slab[0, 0:ENT, :] = ent_s[...]
    wide[0 : 2 * HALF, :] = ent_t[...].astype(F32)
    wide[2 * HALF : 2 * PAD, :] = jnp.zeros((2 * PAD - 2 * HALF, ENT), F32)
    row = lax.broadcasted_iota(jnp.int32, (PAD, ENT), 0)
    slab[0, ENT : ENT + PAD, :] = jnp.where(row < HALF, wide[0:PAD, :], 0.0).astype(BF)
    slab[0, ENT + PAD : BLK, :] = pltpu.roll(wide[...], 2 * PAD - HALF, 0)[0:PAD].astype(BF)
    mids[zh] = jnp.zeros((8, GROUP), jnp.int32)
    mids[zh, 0:3, :] = meta[...]
    pl.semaphore_wait(barrier, len(peers))

    sent = []
    numbers = {}

    def ship(key, src, dst, target):
        n = len(sent)
        numbers[key] = n
        copy = pltpu.make_async_remote_copy(
            src_ref=src,
            dst_ref=dst,
            send_sem=send_sem.at[n],
            recv_sem=recv_sem.at[n],
            device_id=target,
            device_id_type=MESH,
        )
        copy.start()
        sent.append(copy)

    def await_at(key, dst):
        n = numbers[key]
        pltpu.make_async_remote_copy(
            src_ref=dst,
            dst_ref=dst,
            send_sem=send_sem.at[n],
            recv_sem=recv_sem.at[n],
            device_id=mate,
            device_id_type=MESH,
        ).wait_recv()

    def block(k, half=None):
        if half is None:
            return slab.at[k]
        return slab.at[k, pl.ds(half * CUT, CUT), :]

    def push(src, dst, target, half=None):
        ship(("slab", dst, half), block(src, half), block(dst, half), (target, e))

    def got(k, half=None):
        await_at(("slab", k, half), block(k, half))

    def f_start():
        push(slot(0, 0), slot(0, 3), dev(1, 0))
        push(slot(0, 0), slot(0, 1), dev(3, 0))

    def s_start(fd):
        push(slot(0, fd), slot(3, fd), dev(0, 1))
        push(slot(0, fd), slot(1, fd), dev(0, 3))

    def f_step(fd):
        got(slot(0, fd))
        push(slot(0, fd), slot(0, 2), dev(1 if fd == 3 else 3, 0), 0 if fd == 3 else 1)
        s_start(fd)

    def f_last():
        got(slot(0, 2), 0)
        got(slot(0, 2), 1)
        s_start(2)

    def s_step(fd):
        got(slot(3, fd))
        push(slot(3, fd), slot(2, fd), dev(0, 1), 0)
        got(slot(1, fd))
        push(slot(1, fd), slot(2, fd), dev(0, 3), 1)

    lane = lax.broadcasted_iota(jnp.int32, (ROWS, ENT), 1)

    def one_hot(ids, at):
        return jnp.where(ids - at == lane[: ids.shape[0]], 1.0, 0.0).astype(BF)

    def pick(sd, new=False):
        ks = [slot(sd, fd) for fd in range(4)]
        hot = jnp.concatenate(
            [one_hot(idb[...], e * 4096 + dev(fd, sd) * ENT) for fd in range(4)], axis=1
        )
        value = dot_nn(hot, jnp.concatenate([slab[k, 0:ENT, :] for k in ks], axis=0))
        tbuf[4, :, 0:ENT] = value if new else tbuf[4, :, 0:ENT] + value
        for h in range(4):
            lo = ENT + h * 256
            right = jnp.concatenate([slab[k, lo : lo + 256, :] for k in ks], axis=1)
            value = dot_nt(hot, right)
            tbuf[h] = value if new else tbuf[h] + value

    mine = pl.multiple_of(core * GROUP + z * SHARD, SHARD)

    def relations():
        ids = jnp.broadcast_to(mcol[pl.ds(mine, SHARD), 1:2], (SHARD, ENT)).astype(jnp.int32)
        left = REL - RELA
        hot = one_hot(ids, RELA)[:, 0:left]
        racc[...] = jnp.zeros_like(racc)
        racc[:, 0 : 2 * HALF] = dot_nt(hot, rtv[:, RELA:REL])
        rsacc[...] = dot_nn(hot, rsv[RELA:REL, :])

        @pl.loop(0, RELA // 512)
        def _(c):
            at = pl.multiple_of(c * 512, 512)
            hots = jnp.concatenate([one_hot(ids, at + j * ENT) for j in range(4)], axis=1)
            racc[:, 0 : 2 * HALF] += dot_nt(hots, rtv[:, pl.ds(at, 512)])
            rsacc[...] += dot_nn(hots, rsv[pl.ds(at, 512), :])

    f_start()
    s_start(0)
    ship("ids", mids.at[zh], mids.at[zh], zdev(4))
    f_step(3)
    f_step(1)
    await_at("ids", mids.at[1 - zh])
    mrow[...] = jnp.zeros_like(mrow)
    for g in range(2):
        mrow[0:8, :] = mids[g].astype(F32)
        flat = jnp.transpose(mrow[...])
        mcol[g * GROUP : (g + 1) * GROUP, :] = flat
        wanted = jnp.broadcast_to(flat[:, 0:1], (GROUP, ENT)).astype(jnp.int32)
        idb[g * GROUP : (g + 1) * GROUP, :] = wanted
    f_last()
    s_step(0)
    rt_copy.wait()
    rs_copy.wait()
    relations()
    s_step(3)
    s_step(1)
    pick(0, True)
    s_step(2)
    pick(3)
    pick(1)
    for fd in range(4):
        got(slot(2, fd), 0)
        got(slot(2, fd), 1)
    pick(2)

    abuf[:, 0:ENT] = tbuf[4, :, 0:ENT].astype(BF)
    for h in range(4):
        abuf[:, ENT + h * 256 : ENT + (h + 1) * 256] = tbuf[h].astype(BF)
    other = pl.multiple_of((1 - core) * GROUP, GROUP)
    ship("pair", abuf.at[pl.ds(other, GROUP), :], dbuf, mate)
    await_at("pair", dbuf)
    kept = pl.multiple_of(core * GROUP, GROUP)
    sumb[...] = (abuf[pl.ds(kept, GROUP), :].astype(F32) + dbuf[...].astype(F32)).astype(BF)

    def part(d, half):
        return pl.ds(pl.multiple_of(lax.rem(z + d, 8) * SHARD + half * BIT, BIT), BIT)

    def chain(way, role):
        return role if way == 0 else 1 - role

    def ring_send(way, role, j):
        d = j if way == 0 else 8 - j
        rows = part(d, chain(way, role))
        at = way * 7 + role * 4 + (4 - role) - j
        ship(("ring", way, role, j), sumb.at[rows, :], rbuf.at[at], zdev(1 if way == 0 else 7))

    def ring_wait(way, role, j):
        at = way * 7 + role * 4 + (4 - role) - j
        await_at(("ring", way, role, j), rbuf.at[at])
        return rbuf[at].astype(F32)

    for way in range(2):
        ring_send(way, 0, 4)
    for way in range(2):
        ring_send(way, 1, 3)
    for role, j in ((0, 4), (1, 3), (0, 3), (1, 2), (0, 2)):
        for way in range(2):
            came = ring_wait(way, role, j)
            d = j - 1 if way == 0 else 9 - j
            rows = part(d, chain(way, role))
            sumb[rows, :] = (sumb[rows, :].astype(F32) + came).astype(BF)
            ring_send(way, role, j - 1)
    halves = [sumb[part(0, h), :].astype(F32) for h in range(2)]
    for role in (1, 0):
        for way in range(2):
            h = chain(way, role)
            halves[h] = halves[h] + ring_wait(way, role, 1)
    anchor = jnp.concatenate(halves, axis=0)

    sign = 2.0 * mcol[pl.ds(mine, SHARD), 2:3] - 1.0
    a_s, r_s = anchor[:, 0:ENT], rsacc[...]
    a_w, r_w = pltpu.roll(a_s, 64, 1), pltpu.roll(r_s, 64, 1)
    low = lane[:SHARD] < 64
    q_s = jnp.where(low, a_s * r_s - sign * a_w * r_w, a_s * r_w + sign * a_w * r_s)
    a_re, a_im = anchor[:, ENT : ENT + PAD], anchor[:, ENT + PAD : BLK]
    whole = racc[...]
    r_re, r_im = whole[:, 0:PAD], pltpu.roll(whole, 2 * PAD - HALF, 1)[:, 0:PAD]
    qbuf[pl.ds(mine, SHARD), 0:ENT] = q_s.astype(BF)
    qbuf[pl.ds(mine, SHARD), ENT : ENT + PAD] = (a_re * r_re - sign * a_im * r_im).astype(BF)
    qbuf[pl.ds(mine, SHARD), ENT + PAD : BLK] = (a_im * r_re + sign * a_re * r_im).astype(BF)

    def bit(d, half, other=False):
        c = 1 - core if other else core
        at = c * GROUP + lax.rem(z + d, 8) * SHARD + half * BIT
        return qbuf.at[pl.ds(pl.multiple_of(at, BIT), BIT), :]

    def ring_pass(way, role, j):
        d = 8 - (j - 1) if way == 0 else j - 1
        here = bit(d, chain(way, role))
        ship(("pass", way, role, j), here, here, zdev(1 if way == 0 else 7))

    for role in range(2):
        for way in range(2):
            ring_pass(way, role, 1)
    for h in range(2):
        ship(("mate", 0, h), bit(0, h), bit(0, h), mate)
    came = [(0, h) for h in range(2)]
    for role, j in ((0, 1), (1, 1), (0, 2), (1, 2), (0, 3), (1, 3), (0, 4)):
        for way in range(2):
            h = chain(way, role)
            d = 8 - j if way == 0 else j
            await_at(("pass", way, role, j), bit(d, h))
            if j < 4 - role:
                ring_pass(way, role, j + 1)
            ship(("mate", d, h), bit(d, h), bit(d, h), mate)
            came.append((d, h))
    for d, h in came:
        await_at(("mate", d, h), bit(d, h, True))

    mxt[...] = jnp.full_like(mxt, -jnp.inf)
    mxs[...] = jnp.full_like(mxs, -jnp.inf)

    @pl.loop(0, 8)
    def _(p):
        k = 2 * p
        right = jnp.concatenate([slab[k, ENT:BLK, :], slab[k + 1, ENT:BLK, :]], axis=1)
        t = dot_nn(qbuf[:, ENT:BLK], right)
        right = jnp.concatenate([slab[k, 0:ENT, :], slab[k + 1, 0:ENT, :]], axis=0)
        s = dot_nt(qbuf[:, 0:ENT], right)
        tbuf[p] = t
        sbuf[p] = s
        mxt[...] = jnp.maximum(mxt[...], jnp.maximum(t[:, 0:ENT], t[:, ENT:]))
        mxs[...] = jnp.maximum(mxs[...], jnp.maximum(s[:, 0:ENT], s[:, ENT:]))

    mxt[...] = jnp.broadcast_to(jnp.max(mxt[...], axis=1, keepdims=True), (ROWS, ENT))
    mxs[...] = jnp.broadcast_to(jnp.max(mxs[...], axis=1, keepdims=True), (ROWS, ENT))

    @pl.loop(0, ROWS // 64)
    def _(r):
        rows = pl.ds(pl.multiple_of(r * 64, 64), 64)
        top_t, top_s = mxt[rows, :], mxs[rows, :]

        def step(p, carry):
            zt, w, zs = carry
            for h in range(2):
                cols = slice(h * ENT, (h + 1) * ENT)
                t, s = tbuf[p, rows, cols], sbuf[p, rows, cols]
                et, es = jnp.exp(t - top_t), jnp.exp(s - top_s)
                zt, w, zs = zt + et, w + et * (t - s), zs + es
                tbuf[p, rows, cols] = et
                sbuf[p, rows, cols] = es
            return zt, w, zs

        zero = jnp.zeros((64, ENT), F32)
        zt, w, zs = lax.fori_loop(0, 8, step, (zero, zero, zero))
        zt_acc[rows, :] = zt
        w_acc[rows, :] = w
        zs_acc[rows, :] = zs

    table = jnp.where(lane == 0, mxt[...], 0.0)
    table = jnp.where(lane == 1, jnp.sum(zt_acc[...], axis=1, keepdims=True), table)
    table = jnp.where(lane == 2, jnp.sum(w_acc[...], axis=1, keepdims=True), table)
    table = jnp.where(lane == 3, mxs[...], table)
    table = jnp.where(lane == 4, jnp.sum(zs_acc[...], axis=1, keepdims=True), table)
    flat = jnp.transpose(table)[0:8, :]
    own_st[0] = flat[:, 0:GROUP]
    own_st[1] = flat[:, GROUP:ROWS]
    ship("pair stats", own_st.at[1 - core], mate_st, mate)
    qst[...] = jnp.transpose(qbuf[:, 0:ENT].astype(F32)).astype(BF)
    await_at("pair stats", mate_st)

    def merge(tables):
        top_t, top_s = tables[0][0:1, :], tables[0][3:4, :]
        for v in tables[1:]:
            top_t, top_s = jnp.maximum(top_t, v[0:1, :]), jnp.maximum(top_s, v[3:4, :])
        total_t = weighted = total_s = jnp.zeros((1, GROUP), F32)
        for v in tables:
            scale_t, scale_s = jnp.exp(v[0:1, :] - top_t), jnp.exp(v[3:4, :] - top_s)
            total_t = total_t + v[1:2, :] * scale_t
            weighted = weighted + v[2:3, :] * scale_t
            total_s = total_s + v[4:5, :] * scale_s
        return top_t, total_t, weighted, top_s, total_s

    st[z] = jnp.zeros((8, GROUP), F32)
    for i, v in enumerate(merge([own_st[core], mate_st[...]])):
        st[z, i : i + 1, :] = v
    for d in range(1, 8):
        ship(("stats", d), st.at[z], st.at[z], zdev(d))
    for d in range(1, 8):
        await_at(("stats", d), st.at[lax.rem(z + 8 - d, 8)])
    top_t, total_t, weighted, top_s, total_s = merge([st[i] for i in range(8)])
    divergence = weighted / total_t - top_t - jnp.log(total_t) + top_s + jnp.log(total_s)
    fin[core] = jnp.zeros((8, GROUP), F32)
    for i, v in enumerate((top_t, total_t, divergence, top_s, total_s)):
        fin[core, i : i + 1, :] = v
    ship("final", fin.at[core], fin.at[core], mate)
    await_at("final", fin.at[1 - core])
    div_out[...] = fin[zh, 2:3, :]
    rowi = lax.broadcasted_iota(jnp.int32, (ENT, GROUP), 0)
    for g in range(2):
        f_t = jnp.exp(own_st[g, 0:1, :] - fin[g, 0:1, :]) / fin[g, 1:2, :]
        f_s = jnp.exp(own_st[g, 3:4, :] - fin[g, 3:4, :]) / fin[g, 4:5, :]
        flipped = jnp.transpose(jnp.where(rowi == 0, f_t, jnp.where(rowi == 1, f_s, 0.0)))
        ftb[g * GROUP : (g + 1) * GROUP, :] = jnp.broadcast_to(flipped[:, 0:1], (GROUP, ENT))
        fsb[g * GROUP : (g + 1) * GROUP, :] = jnp.broadcast_to(flipped[:, 1:2], (GROUP, ENT))

    qg[...] = jnp.zeros_like(qg)
    for sd in (2, 1, 3, 0):

        @pl.loop(0, 2)
        def _(i, sd=sd):
            p = sd * 2 + i
            halves = []
            for h in range(2):
                cols = slice(h * ENT, (h + 1) * ENT)
                g = sbuf[p, :, cols] * fsb[...] - tbuf[p, :, cols] * ftb[...]
                halves.append(g.astype(BF))
            g = jnp.concatenate(halves, axis=1)
            grad = dot_nn(qst[...], g)
            for h in range(2):
                cols = slice(h * ENT, (h + 1) * ENT)
                if sd:
                    eg_s[sd - 1, 2 * i + h] = grad[:, cols].astype(BF)
                else:
                    eg_own[2 * i + h] = grad[:, cols]
            right = jnp.concatenate([slab[2 * p, 0:ENT, :], slab[2 * p + 1, 0:ENT, :]], axis=0)
            qg[...] += dot_nn(g, right)

        if sd:
            ship(("second", sd), eg_s.at[sd - 1], eg_sr.at[sd - 1], (dev(0, sd), e))

    qgb[...] = qg[pl.ds(other, GROUP), :].astype(BF)
    ship("pair grad", qgb, qgd, mate)
    for sd in (1, 3, 2):
        await_at(("second", sd), eg_sr.at[sd - 1])
    for fd in (2, 1, 3, 0):
        v = eg_own[fd]
        for sd in (1, 2, 3):
            v = v + eg_sr[sd - 1, fd].astype(F32)
        if fd:
            eg_f[fd - 1] = v.astype(BF)
            ship(("first", fd), eg_f.at[fd - 1], eg_fr.at[fd - 1], (dev(fd, 0), e))
        else:
            near = v
    await_at("pair grad", qgd)
    qgsum[...] = qg[pl.ds(kept, GROUP), :] + qgd[...].astype(F32)
    qgz[...] = qgsum[...].astype(BF)
    for d in range(1, 8):
        at = pl.multiple_of(lax.rem(z + d, 8) * SHARD, SHARD)
        ship(("shard", d), qgz.at[pl.ds(at, SHARD), :], qgr.at[d - 1], zdev(d))
    for fd in (1, 3, 2):
        await_at(("first", fd), eg_fr.at[fd - 1])
    for fd in (1, 2, 3):
        near = near + eg_fr[fd - 1].astype(F32)
    eg_out[...] = jnp.transpose(near)
    total = qgsum[pl.ds(pl.multiple_of(z * SHARD, SHARD), SHARD), :]
    for d in range(1, 8):
        await_at(("shard", d), qgr.at[d - 1])
    for d in range(1, 8):
        total = total + qgr[d - 1].astype(F32)

    def out_rows(d):
        return qgo.at[core, pl.ds(pl.multiple_of(lax.rem(z + d, 8) * SHARD, SHARD), SHARD), :]

    qgo[core, pl.ds(pl.multiple_of(z * SHARD, SHARD), SHARD), :] = total.astype(BF)
    for d in range(1, 8):
        ship(("sum", d), out_rows(0), out_rows(0), zdev(d))
    for d in range(1, 8):
        await_at(("sum", d), out_rows(8 - d))
    ship("pair sum", qgo.at[core], qgo.at[core], mate)
    await_at("pair sum", qgo.at[1 - core])
    qg_out[...] = qgo[zh].astype(F32)

    for copy in sent:
        copy.wait_send()


def per_device(
    anchor_ids,
    relation_ids,
    side_flags,
    teacher_entities,
    student_entities,
    teacher_relations,
    student_relations,
):
    meta = jnp.stack([anchor_ids, relation_ids, side_flags], axis=0)
    vmem = pl.BlockSpec(memory_space=pltpu.VMEM)
    hbm = pl.BlockSpec(memory_space=pl.ANY)
    big = (ROWS, ENT)
    div, eg, qg = pl.pallas_call(
        kernel,
        out_shape=(
            jax.ShapeDtypeStruct((1, GROUP), F32),
            jax.ShapeDtypeStruct((ENT, ENT), F32),
            jax.ShapeDtypeStruct((GROUP, ENT), F32),
        ),
        in_specs=[vmem, vmem, vmem, hbm, hbm],
        out_specs=(vmem, vmem, vmem),
        scratch_shapes=[
            pltpu.VMEM((16, BLK, ENT), BF),
            pltpu.VMEM((2 * HALF, REL), BF),
            pltpu.VMEM((REL, ENT), BF),
            pltpu.VMEM((2 * PAD, ENT), F32),
            pltpu.VMEM((2, 8, GROUP), jnp.int32),
            pltpu.VMEM((ENT, GROUP), F32),
            pltpu.VMEM(big, F32),
            pltpu.VMEM(big, jnp.int32),
            pltpu.VMEM((ROWS, BLK), BF),
            pltpu.VMEM((GROUP, BLK), BF),
            pltpu.VMEM((GROUP, BLK), BF),
            pltpu.VMEM((14, BIT, BLK), BF),
            pltpu.VMEM((SHARD, 2 * PAD), F32),
            pltpu.VMEM((SHARD, ENT), F32),
            pltpu.VMEM((ROWS, BLK), BF),
            pltpu.VMEM((8, ROWS, 256), F32),
            pltpu.VMEM((8, ROWS, 256), F32),
            pltpu.VMEM(big, F32),
            pltpu.VMEM(big, F32),
            pltpu.VMEM(big, F32),
            pltpu.VMEM(big, F32),
            pltpu.VMEM(big, F32),
            pltpu.VMEM((2, 8, GROUP), F32),
            pltpu.VMEM((8, GROUP), F32),
            pltpu.VMEM((8, 8, GROUP), F32),
            pltpu.VMEM((2, 8, GROUP), F32),
            pltpu.VMEM(big, F32),
            pltpu.VMEM(big, F32),
            pltpu.VMEM((ENT, ROWS), BF),
            pltpu.VMEM((4, ENT, ENT), F32),
            pltpu.VMEM((3, 4, ENT, ENT), BF),
            pltpu.VMEM((3, 4, ENT, ENT), BF),
            pltpu.VMEM((3, ENT, ENT), BF),
            pltpu.VMEM((3, ENT, ENT), BF),
            pltpu.VMEM(big, F32),
            pltpu.VMEM((GROUP, ENT), BF),
            pltpu.VMEM((GROUP, ENT), BF),
            pltpu.VMEM((GROUP, ENT), F32),
            pltpu.VMEM((GROUP, ENT), BF),
            pltpu.VMEM((7, SHARD, ENT), BF),
            pltpu.VMEM((2, GROUP, ENT), BF),
            pltpu.SemaphoreType.DMA((2,)),
            pltpu.SemaphoreType.DMA((110,)),
            pltpu.SemaphoreType.DMA((110,)),
        ],
        compiler_params=pltpu.CompilerParams(
            collective_id=0, has_side_effects=True, vmem_limit_bytes=60 * 2**20
        ),
    )(meta, teacher_entities.T, student_entities, teacher_relations.T, student_relations)
    return div.reshape(GROUP), eg, qg


def solution(mesh):
    in_specs = (
        P("query"),
        P("query"),
        P("query"),
        P(("entity", "query"), None),
        P(("entity", "query"), None),
        P(),
        P(),
    )
    out_specs = (P("query"), P(("entity", "query"), None), P("query", None))
    return jax.shard_map(
        per_device, mesh=mesh, in_specs=in_specs, out_specs=out_specs, check_vma=False
    )
```

```python
import jax
import jax.numpy as jnp
from jax import lax
from jax.experimental import pallas as pl
from jax.experimental.pallas import tpu as pltpu
from jax.sharding import PartitionSpec as P

MESH = pl.DeviceIdType.MESH
BF = jnp.bfloat16
F32 = jnp.float32
GROUP = 512
ROWS = 2 * GROUP
ENT = 128
HALF = 500
PAD = 512
BLK = ENT + 2 * PAD
CUT = BLK // 2
REL = 4131
RELA = 4096
SHARD = 64
BIT = 32


def slot(sd, fd):
    return sd * 4 + fd


def dot_nn(a, b):
    return lax.dot_general(a, b, (((1,), (0,)), ((), ())), preferred_element_type=F32)


def dot_nt(a, b):
    return lax.dot_general(a, b, (((1,), (1,)), ((), ())), preferred_element_type=F32)


def kernel(
    anchors,
    relation_ids,
    flags,
    ent_t,
    ent_s,
    rel_t,
    rel_s,
    div_out,
    eg_out,
    qg_out,
    slab,
    rtv,
    rsv,
    wide,
    mids,
    mrow,
    mcol,
    idb,
    abuf,
    dbuf,
    sumb,
    rbuf,
    racc,
    rsacc,
    qbuf,
    tbuf,
    sbuf,
    mxt,
    mxs,
    zt_acc,
    w_acc,
    zs_acc,
    own_st,
    mate_st,
    st,
    fin,
    ftb,
    fsb,
    qst,
    gbuf,
    eg_own,
    eg_s,
    eg_sr,
    eg_f,
    eg_fr,
    qg,
    qgb,
    qgd,
    qgsum,
    qgz,
    qgr,
    qgo,
    idv,
    ent_v,
    ens_v,
    loc_sem,
    send_sem,
    recv_sem,
):
    q = lax.axis_index("query")
    e = lax.axis_index("entity")
    x, zh, y = lax.div(q, 8), lax.rem(lax.div(q, 4), 2), lax.rem(q, 4)
    zl, core = lax.div(e, 2), lax.rem(e, 2)
    z = zh * 4 + zl
    first = x + core * (y - x)
    second = y + core * (x - y)

    def dev(fd, sd):
        a, b = lax.rem(first + fd, 4), lax.rem(second + sd, 4)
        return (a + core * (b - a)) * 8 + zh * 4 + b + core * (a - b)

    def zdev(d):
        zz = lax.rem(z + d, 8)
        return (x * 8 + lax.div(zz, 4) * 4 + y, lax.rem(zz, 4) * 2 + core)

    mate = (q, zl * 2 + 1 - core)

    moves = ((ent_t, ent_v), (ent_s, ens_v), (anchors, idv.at[0]), (relation_ids, idv.at[1]), (flags, idv.at[2]))
    moves = [pltpu.make_async_copy(a, b, loc_sem.at[2 + i]) for i, (a, b) in enumerate(moves)]
    for move in moves:
        move.start()

    barrier = pltpu.get_barrier_semaphore()
    peers = [(dev(d, 0), e) for d in (1, 2, 3)]
    peers += [(dev(0, d), e) for d in (1, 2, 3)]
    peers += [zdev(d) for d in range(1, 8)]
    peers += [mate]
    for peer in peers:
        pl.semaphore_signal(barrier, inc=1, device_id=peer, device_id_type=MESH)

    rt_copy = pltpu.make_async_copy(rel_t, rtv, loc_sem.at[0])
    rs_copy = pltpu.make_async_copy(rel_s, rsv, loc_sem.at[1])
    for move in moves:
        move.wait()

    slab[0, 0:ENT, :] = ens_v[...]
    wide[0 : 2 * HALF, :] = ent_v[...].astype(F32)
    wide[2 * HALF : 2 * PAD, :] = jnp.zeros((2 * PAD - 2 * HALF, ENT), F32)
    row = lax.broadcasted_iota(jnp.int32, (PAD, ENT), 0)
    slab[0, ENT : ENT + PAD, :] = jnp.where(row < HALF, wide[0:PAD, :], 0.0).astype(BF)
    slab[0, ENT + PAD : BLK, :] = pltpu.roll(wide[...], 2 * PAD - HALF, 0)[0:PAD].astype(BF)
    mids[zh] = jnp.zeros((8, GROUP), jnp.int32)
    for i in range(3):
        mids[zh, i : i + 1, :] = idv[i]
    rt_copy.start()
    rs_copy.start()
    pl.semaphore_wait(barrier, len(peers))

    sent = []
    numbers = {}

    def ship(key, src, dst, target):
        n = len(sent)
        numbers[key] = n
        copy = pltpu.make_async_remote_copy(
            src_ref=src,
            dst_ref=dst,
            send_sem=send_sem.at[n],
            recv_sem=recv_sem.at[n],
            device_id=target,
            device_id_type=MESH,
        )
        copy.start()
        sent.append(copy)

    def await_at(key, dst):
        n = numbers[key]
        pltpu.make_async_remote_copy(
            src_ref=dst,
            dst_ref=dst,
            send_sem=send_sem.at[n],
            recv_sem=recv_sem.at[n],
            device_id=mate,
            device_id_type=MESH,
        ).wait_recv()

    def block(k, half):
        return slab.at[k, pl.ds(half * CUT, CUT), :]

    def push(src, dst, target, half):
        ship(("slab", dst, half), block(src, half), block(dst, half), (target, e))

    def got(k, half):
        await_at(("slab", k, half), block(k, half))

    def f_start():
        for up, down in ((0, 1), (1, 0)):
            push(slot(0, 0), slot(0, 3), dev(1, 0), up)
            push(slot(0, 0), slot(0, 1), dev(3, 0), down)

    def s_start(fd, half):
        for sd in (1, 3) if half == 0 else (3, 1):
            push(slot(0, fd), slot(4 - sd, fd), dev(0, sd), half)

    def f_turn():
        got(slot(0, 3), 0)
        push(slot(0, 3), slot(0, 2), dev(1, 0), 0)
        got(slot(0, 1), 1)
        push(slot(0, 1), slot(0, 2), dev(3, 0), 1)
        s_start(3, 0)
        s_start(1, 1)
        got(slot(0, 3), 1)
        s_start(3, 1)
        got(slot(0, 1), 0)
        s_start(1, 0)

    def f_last():
        for half in range(2):
            got(slot(0, 2), half)
            s_start(2, half)

    def s_turn(fd):
        got(slot(3, fd), 0)
        push(slot(3, fd), slot(2, fd), dev(0, 1), 0)
        got(slot(1, fd), 1)
        push(slot(1, fd), slot(2, fd), dev(0, 3), 1)

    def s_rest():
        for fd in (0, 3, 1, 2):
            got(slot(3, fd), 1)
            got(slot(1, fd), 0)

    lane = lax.broadcasted_iota(jnp.int32, (ROWS, ENT), 1)

    def one_hot(ids, at):
        return jnp.where(ids - at == lane[: ids.shape[0]], 1.0, 0.0).astype(BF)

    def pick(sd, new=False, fds=(0, 1, 2, 3)):
        ks = [slot(sd, fd) for fd in fds]
        hot = jnp.concatenate(
            [one_hot(idb[...], e * 4096 + dev(fd, sd) * ENT) for fd in fds], axis=1
        )
        value = dot_nn(hot, jnp.concatenate([slab[k, 0:ENT, :] for k in ks], axis=0))
        tbuf[4, :, 0:ENT] = value if new else tbuf[4, :, 0:ENT] + value
        for h in range(4):
            lo = ENT + h * 256
            right = jnp.concatenate([slab[k, lo : lo + 256, :] for k in ks], axis=1)
            value = dot_nt(hot, right)
            tbuf[h] = value if new else tbuf[h] + value

    mine = pl.multiple_of(core * GROUP + z * SHARD, SHARD)

    def relations():
        ids = jnp.broadcast_to(mcol[pl.ds(mine, SHARD), 1:2], (SHARD, ENT)).astype(jnp.int32)
        left = REL - RELA
        hot = one_hot(ids, RELA)[:, 0:left]
        racc[...] = jnp.zeros_like(racc)
        racc[:, 0 : 2 * HALF] = dot_nt(hot, rtv[:, RELA:REL])
        rsacc[...] = dot_nn(hot, rsv[RELA:REL, :])

        @pl.loop(0, RELA // 512)
        def _(c):
            at = pl.multiple_of(c * 512, 512)
            hots = jnp.concatenate([one_hot(ids, at + j * ENT) for j in range(4)], axis=1)
            racc[:, 0 : 2 * HALF] += dot_nt(hots, rtv[:, pl.ds(at, 512)])
            rsacc[...] += dot_nn(hots, rsv[pl.ds(at, 512), :])

    f_start()
    s_start(0, 0)
    s_start(0, 1)
    ship("ids", mids.at[zh], mids.at[zh], zdev(4))
    f_turn()
    s_turn(0)
    await_at("ids", mids.at[1 - zh])
    mrow[...] = jnp.zeros_like(mrow)
    for g in range(2):
        mrow[0:8, :] = mids[g].astype(F32)
        flat = jnp.transpose(mrow[...])
        mcol[g * GROUP : (g + 1) * GROUP, :] = flat
        wanted = jnp.broadcast_to(flat[:, 0:1], (GROUP, ENT)).astype(jnp.int32)
        idb[g * GROUP : (g + 1) * GROUP, :] = wanted
    f_last()
    s_turn(3)
    s_turn(1)
    rt_copy.wait()
    rs_copy.wait()
    pick(0, True)
    s_turn(2)
    relations()
    s_rest()
    pick(3)
    pick(1)
    for fds in ((0, 3), (1, 2)):
        for fd in fds:
            got(slot(2, fd), 0)
            got(slot(2, fd), 1)
        pick(2, fds=fds)

    def shard(d, c=None):
        at = lax.rem(z + d, 8) * SHARD
        return pl.ds(pl.multiple_of(at if c is None else c * GROUP + at, SHARD), SHARD)

    order = (4, 3, 5, 2, 6, 1, 7, 0)
    for d in order:
        theirs = shard(d, 1 - core)
        abuf[shard(d), 0:ENT] = tbuf[4, theirs, 0:ENT].astype(BF)
        for h in range(4):
            abuf[shard(d), ENT + h * 256 : ENT + (h + 1) * 256] = tbuf[h, theirs, :].astype(BF)
        ship(("pair", d), abuf.at[shard(d), :], dbuf.at[shard(d), :], mate)

    def merge_cores(d):
        await_at(("pair", d), dbuf.at[shard(d), :])
        came = dbuf[shard(d), :].astype(F32)
        ours = shard(d, core)
        sumb[shard(d), 0:ENT] = (tbuf[4, ours, 0:ENT] + came[:, 0:ENT]).astype(BF)
        for h in range(4):
            cols = slice(ENT + h * 256, ENT + (h + 1) * 256)
            sumb[shard(d), cols] = (tbuf[h, ours, :] + came[:, cols]).astype(BF)

    def part(d, half):
        return pl.ds(pl.multiple_of(lax.rem(z + d, 8) * SHARD + half * BIT, BIT), BIT)

    def chain(way, role):
        return role if way == 0 else 1 - role

    def ring_send(way, role, j):
        d = j if way == 0 else 8 - j
        rows = part(d, chain(way, role))
        at = way * 7 + role * 4 + (4 - role) - j
        ship(("ring", way, role, j), sumb.at[rows, :], rbuf.at[at], zdev(1 if way == 0 else 7))

    def ring_wait(way, role, j):
        at = way * 7 + role * 4 + (4 - role) - j
        await_at(("ring", way, role, j), rbuf.at[at])
        return rbuf[at].astype(F32)

    merge_cores(4)
    for way in range(2):
        ring_send(way, 0, 4)
    for way in range(2):
        merge_cores(3 if way == 0 else 5)
        ring_send(way, 1, 3)
    for d in order[3:]:
        merge_cores(d)
    for role, j in ((0, 4), (1, 3), (0, 3), (1, 2), (0, 2)):
        for way in range(2):
            came = ring_wait(way, role, j)
            d = j - 1 if way == 0 else 9 - j
            rows = part(d, chain(way, role))
            sumb[rows, :] = (sumb[rows, :].astype(F32) + came).astype(BF)
            ring_send(way, role, j - 1)
    halves = [sumb[part(0, h), :].astype(F32) for h in range(2)]
    for role in (1, 0):
        for way in range(2):
            h = chain(way, role)
            halves[h] = halves[h] + ring_wait(way, role, 1)
    anchor = jnp.concatenate(halves, axis=0)

    sign = 2.0 * mcol[pl.ds(mine, SHARD), 2:3] - 1.0
    a_s, r_s = anchor[:, 0:ENT], rsacc[...]
    a_w, r_w = pltpu.roll(a_s, 64, 1), pltpu.roll(r_s, 64, 1)
    low = lane[:SHARD] < 64
    q_s = jnp.where(low, a_s * r_s - sign * a_w * r_w, a_s * r_w + sign * a_w * r_s)
    a_re, a_im = anchor[:, ENT : ENT + PAD], anchor[:, ENT + PAD : BLK]
    whole = racc[...]
    r_re, r_im = whole[:, 0:PAD], pltpu.roll(whole, 2 * PAD - HALF, 1)[:, 0:PAD]
    qbuf[pl.ds(mine, SHARD), 0:ENT] = q_s.astype(BF)
    qbuf[pl.ds(mine, SHARD), ENT : ENT + PAD] = (a_re * r_re - sign * a_im * r_im).astype(BF)
    qbuf[pl.ds(mine, SHARD), ENT + PAD : BLK] = (a_im * r_re + sign * a_re * r_im).astype(BF)

    def bit(d, half, other=False):
        c = 1 - core if other else core
        at = c * GROUP + lax.rem(z + d, 8) * SHARD + half * BIT
        return qbuf.at[pl.ds(pl.multiple_of(at, BIT), BIT), :]

    def ring_pass(way, role, j):
        d = 8 - (j - 1) if way == 0 else j - 1
        here = bit(d, chain(way, role))
        ship(("pass", way, role, j), here, here, zdev(1 if way == 0 else 7))

    for role in range(2):
        for way in range(2):
            ring_pass(way, role, 1)
    for h in range(2):
        ship(("mate", 0, h), bit(0, h), bit(0, h), mate)

    def pass_on(role, j):
        for way in range(2):
            h = chain(way, role)
            d = 8 - j if way == 0 else j
            await_at(("pass", way, role, j), bit(d, h))
            if j < 3:
                ring_pass(way, role, j + 1)
            if (role, j) == (0, 2):
                ship(("pass", way, 0, 4), bit(d, h), bit(d, h), zdev(2 if way == 0 else 6))
            ship(("mate", d, h), bit(d, h), bit(d, h), mate)

    def score(start, stride, number):
        ds = [(start + stride * i) % 8 for i in range(number)]
        for d in ds:
            for h in range(2):
                await_at(("mate", d, h), bit(d, h, True))

        def rows_at(g, d):
            return pl.ds(pl.multiple_of(g * GROUP + lax.rem(z + d, 8) * SHARD, SHARD), SHARD)

        pieces = [rows_at(g, d) for g in range(2) for d in ds]
        for rows in pieces:
            mxt[rows, :] = jnp.full((SHARD, ENT), -jnp.inf)
            mxs[rows, :] = jnp.full((SHARD, ENT), -jnp.inf)

        @pl.loop(0, 8)
        def _(p):
            k = 2 * p
            left = jnp.concatenate([qbuf[rows, :] for rows in pieces], axis=0)
            right = jnp.concatenate([slab[k, ENT:BLK, :], slab[k + 1, ENT:BLK, :]], axis=1)
            t = dot_nn(left[:, ENT:BLK], right)
            right = jnp.concatenate([slab[k, 0:ENT, :], slab[k + 1, 0:ENT, :]], axis=0)
            s = dot_nt(left[:, 0:ENT], right)
            for i, rows in enumerate(pieces):
                ti, si = t[i * SHARD : (i + 1) * SHARD], s[i * SHARD : (i + 1) * SHARD]
                tbuf[p, rows, :] = ti
                sbuf[p, rows, :] = si
                mxt[rows, :] = jnp.maximum(mxt[rows, :], jnp.maximum(ti[:, 0:ENT], ti[:, ENT:]))
                mxs[rows, :] = jnp.maximum(mxs[rows, :], jnp.maximum(si[:, 0:ENT], si[:, ENT:]))

        @pl.loop(0, 2 * number)
        def _(r):
            g = lax.div(r, number)
            rows = rows_at(g, start + stride * (r - g * number))
            top_t = jnp.broadcast_to(jnp.max(mxt[rows, :], axis=1, keepdims=True), (SHARD, ENT))
            top_s = jnp.broadcast_to(jnp.max(mxs[rows, :], axis=1, keepdims=True), (SHARD, ENT))
            mxt[rows, :] = top_t
            mxs[rows, :] = top_s

            def step(p, carry):
                zt, w, zs = carry
                for h in range(2):
                    cols = slice(h * ENT, (h + 1) * ENT)
                    t, s = tbuf[p, rows, cols], sbuf[p, rows, cols]
                    et, es = jnp.exp(t - top_t), jnp.exp(s - top_s)
                    zt, w, zs = zt + et, w + et * (t - s), zs + es
                    tbuf[p, rows, cols] = et
                    sbuf[p, rows, cols] = es
                return zt, w, zs

            zero = jnp.zeros((SHARD, ENT), F32)
            zt, w, zs = lax.fori_loop(0, 8, step, (zero, zero, zero))
            zt_acc[rows, :] = zt
            w_acc[rows, :] = w
            zs_acc[rows, :] = zs

    for role, j in ((0, 1), (1, 1), (0, 2), (1, 2)):
        pass_on(role, j)
    score(6, 1, 5)
    for role, j in ((0, 3), (1, 3), (0, 4)):
        pass_on(role, j)
    score(3, 1, 3)

    table = jnp.where(lane == 0, mxt[...], 0.0)
    table = jnp.where(lane == 1, jnp.sum(zt_acc[...], axis=1, keepdims=True), table)
    table = jnp.where(lane == 2, jnp.sum(w_acc[...], axis=1, keepdims=True), table)
    table = jnp.where(lane == 3, mxs[...], table)
    table = jnp.where(lane == 4, jnp.sum(zs_acc[...], axis=1, keepdims=True), table)
    flat = jnp.transpose(table)[0:8, :]
    own_st[0] = flat[:, 0:GROUP]
    own_st[1] = flat[:, GROUP:ROWS]
    ship("pair stats", own_st.at[1 - core], mate_st, mate)
    qst[...] = jnp.transpose(qbuf[:, 0:ENT].astype(F32)).astype(BF)
    await_at("pair stats", mate_st)

    def merge(tables):
        top_t, top_s = tables[0][0:1, :], tables[0][3:4, :]
        for v in tables[1:]:
            top_t, top_s = jnp.maximum(top_t, v[0:1, :]), jnp.maximum(top_s, v[3:4, :])
        total_t = weighted = total_s = jnp.zeros((1, GROUP), F32)
        for v in tables:
            scale_t, scale_s = jnp.exp(v[0:1, :] - top_t), jnp.exp(v[3:4, :] - top_s)
            total_t = total_t + v[1:2, :] * scale_t
            weighted = weighted + v[2:3, :] * scale_t
            total_s = total_s + v[4:5, :] * scale_s
        return top_t, total_t, weighted, top_s, total_s

    st[z] = jnp.zeros((8, GROUP), F32)
    for i, v in enumerate(merge([own_st[core], mate_st[...]])):
        st[z, i : i + 1, :] = v
    for d in range(1, 8):
        ship(("stats", d), st.at[z], st.at[z], zdev(d))
    for d in range(1, 8):
        await_at(("stats", d), st.at[lax.rem(z + 8 - d, 8)])
    top_t, total_t, weighted, top_s, total_s = merge([st[i] for i in range(8)])
    divergence = weighted / total_t - top_t - jnp.log(total_t) + top_s + jnp.log(total_s)
    fin[core] = jnp.zeros((8, GROUP), F32)
    for i, v in enumerate((top_t, total_t, divergence, top_s, total_s)):
        fin[core, i : i + 1, :] = v
    ship("final", fin.at[core], fin.at[core], mate)
    await_at("final", fin.at[1 - core])
    div_out[...] = fin[zh, 2:3, :]
    rowi = lax.broadcasted_iota(jnp.int32, (ENT, GROUP), 0)
    for g in range(2):
        f_t = jnp.exp(own_st[g, 0:1, :] - fin[g, 0:1, :]) / fin[g, 1:2, :]
        f_s = jnp.exp(own_st[g, 3:4, :] - fin[g, 3:4, :]) / fin[g, 4:5, :]
        flipped = jnp.transpose(jnp.where(rowi == 0, f_t, jnp.where(rowi == 1, f_s, 0.0)))
        ftb[g * GROUP : (g + 1) * GROUP, :] = jnp.broadcast_to(flipped[:, 0:1], (GROUP, ENT))
        fsb[g * GROUP : (g + 1) * GROUP, :] = jnp.broadcast_to(flipped[:, 1:2], (GROUP, ENT))

    qg[...] = jnp.zeros_like(qg)

    @pl.loop(0, 8)
    def _(p):
        halves = []
        for h in range(2):
            cols = slice(h * ENT, (h + 1) * ENT)
            g = sbuf[p, :, cols] * fsb[...] - tbuf[p, :, cols] * ftb[...]
            halves.append(g.astype(BF))
        g = jnp.concatenate(halves, axis=1)
        gbuf[p] = g
        right = jnp.concatenate([slab[2 * p, 0:ENT, :], slab[2 * p + 1, 0:ENT, :]], axis=0)
        qg[...] += dot_nn(g, right)

    other = pl.multiple_of((1 - core) * GROUP, GROUP)
    kept = pl.multiple_of(core * GROUP, GROUP)
    qgb[...] = qg[pl.ds(other, GROUP), :].astype(BF)
    ship("pair grad", qgb, qgd, mate)

    def entities(sd):
        @pl.loop(0, 2)
        def _(i):
            grad = dot_nn(qst[...], gbuf[sd * 2 + i])
            for h in range(2):
                cols = slice(h * ENT, (h + 1) * ENT)
                if sd:
                    eg_s[sd - 1, 2 * i + h] = grad[:, cols].astype(BF)
                else:
                    eg_own[2 * i + h] = grad[:, cols]

        if sd:
            ship(("second", sd), eg_s.at[sd - 1], eg_sr.at[sd - 1], (dev(0, sd), e))

    entities(2)
    entities(1)
    await_at("pair grad", qgd)
    qgsum[...] = qg[pl.ds(kept, GROUP), :] + qgd[...].astype(F32)
    qgz[...] = qgsum[...].astype(BF)
    for d in range(1, 8):
        at = pl.multiple_of(lax.rem(z + d, 8) * SHARD, SHARD)
        ship(("shard", d), qgz.at[pl.ds(at, SHARD), :], qgr.at[d - 1], zdev(d))
    entities(3)
    entities(0)
    for sd in (1, 3, 2):
        await_at(("second", sd), eg_sr.at[sd - 1])
    for fd in (2, 1, 3, 0):
        v = eg_own[fd]
        for sd in (1, 2, 3):
            v = v + eg_sr[sd - 1, fd].astype(F32)
        if fd:
            eg_f[fd - 1] = v.astype(BF)
            ship(("first", fd), eg_f.at[fd - 1], eg_fr.at[fd - 1], (dev(fd, 0), e))
        else:
            near = v
    total = qgsum[pl.ds(pl.multiple_of(z * SHARD, SHARD), SHARD), :]
    for d in range(1, 8):
        await_at(("shard", d), qgr.at[d - 1])
    for d in range(1, 8):
        total = total + qgr[d - 1].astype(F32)

    def out_rows(d):
        return qgo.at[core, pl.ds(pl.multiple_of(lax.rem(z + d, 8) * SHARD, SHARD), SHARD), :]

    qgo[core, pl.ds(pl.multiple_of(z * SHARD, SHARD), SHARD), :] = total.astype(BF)
    for d in range(1, 8):
        ship(("sum", d), out_rows(0), out_rows(0), zdev(d))
    for fd in (1, 3, 2):
        await_at(("first", fd), eg_fr.at[fd - 1])
    for fd in (1, 2, 3):
        near = near + eg_fr[fd - 1].astype(F32)
    eg_out[...] = jnp.transpose(near)
    for d in range(1, 8):
        await_at(("sum", d), out_rows(8 - d))
    ship("pair sum", qgo.at[core], qgo.at[core], mate)
    await_at("pair sum", qgo.at[1 - core])
    qg_out[...] = qgo[zh].astype(F32)

    for copy in sent:
        copy.wait_send()


def finish(div, eg, qg, div_out, eg_out, qg_out):
    div_out[...] = div[...]
    eg_out[...] = eg[...]
    qg_out[...] = qg[...]


def per_device(
    anchor_ids,
    relation_ids,
    side_flags,
    teacher_entities,
    student_entities,
    teacher_relations,
    student_relations,
):
    rows = [v.reshape(1, GROUP) for v in (anchor_ids, relation_ids, side_flags)]
    vmem = pl.BlockSpec(memory_space=pltpu.VMEM)
    hbm = pl.BlockSpec(memory_space=pl.ANY)
    big = (ROWS, ENT)
    div, eg, qg = pl.pallas_call(
        kernel,
        out_shape=(
            jax.ShapeDtypeStruct((1, GROUP), F32),
            jax.ShapeDtypeStruct((ENT, ENT), F32),
            jax.ShapeDtypeStruct((GROUP, ENT), F32),
        ),
        in_specs=[hbm] * 7,
        out_specs=(vmem, vmem, vmem),
        scratch_shapes=[
            pltpu.VMEM((16, BLK, ENT), BF),
            pltpu.VMEM((2 * HALF, REL), BF),
            pltpu.VMEM((REL, ENT), BF),
            pltpu.VMEM((2 * PAD, ENT), F32),
            pltpu.VMEM((2, 8, GROUP), jnp.int32),
            pltpu.VMEM((ENT, GROUP), F32),
            pltpu.VMEM(big, F32),
            pltpu.VMEM(big, jnp.int32),
            pltpu.VMEM((GROUP, BLK), BF),
            pltpu.VMEM((GROUP, BLK), BF),
            pltpu.VMEM((GROUP, BLK), BF),
            pltpu.VMEM((14, BIT, BLK), BF),
            pltpu.VMEM((SHARD, 2 * PAD), F32),
            pltpu.VMEM((SHARD, ENT), F32),
            pltpu.VMEM((ROWS, BLK), BF),
            pltpu.VMEM((8, ROWS, 256), F32),
            pltpu.VMEM((8, ROWS, 256), F32),
            pltpu.VMEM(big, F32),
            pltpu.VMEM(big, F32),
            pltpu.VMEM(big, F32),
            pltpu.VMEM(big, F32),
            pltpu.VMEM(big, F32),
            pltpu.VMEM((2, 8, GROUP), F32),
            pltpu.VMEM((8, GROUP), F32),
            pltpu.VMEM((8, 8, GROUP), F32),
            pltpu.VMEM((2, 8, GROUP), F32),
            pltpu.VMEM(big, F32),
            pltpu.VMEM(big, F32),
            pltpu.VMEM((ENT, ROWS), BF),
            pltpu.VMEM((8, ROWS, 256), BF),
            pltpu.VMEM((4, ENT, ENT), F32),
            pltpu.VMEM((3, 4, ENT, ENT), BF),
            pltpu.VMEM((3, 4, ENT, ENT), BF),
            pltpu.VMEM((3, ENT, ENT), BF),
            pltpu.VMEM((3, ENT, ENT), BF),
            pltpu.VMEM(big, F32),
            pltpu.VMEM((GROUP, ENT), BF),
            pltpu.VMEM((GROUP, ENT), BF),
            pltpu.VMEM((GROUP, ENT), F32),
            pltpu.VMEM((GROUP, ENT), BF),
            pltpu.VMEM((7, SHARD, ENT), BF),
            pltpu.VMEM((2, GROUP, ENT), BF),
            pltpu.VMEM((3, 1, GROUP), jnp.int32),
            pltpu.VMEM((2 * HALF, ENT), BF),
            pltpu.VMEM((ENT, ENT), BF),
            pltpu.SemaphoreType.DMA((7,)),
            pltpu.SemaphoreType.DMA((120,)),
            pltpu.SemaphoreType.DMA((120,)),
        ],
        compiler_params=pltpu.CompilerParams(
            collective_id=0, has_side_effects=True, vmem_limit_bytes=60 * 2**20
        ),
    )(*rows, teacher_entities.T, student_entities, teacher_relations.T, student_relations)
    div, eg, qg = pl.pallas_call(
        finish,
        out_shape=(
            jax.ShapeDtypeStruct((1, GROUP), F32),
            jax.ShapeDtypeStruct((ENT, ENT), F32),
            jax.ShapeDtypeStruct((GROUP, ENT), F32),
        ),
        in_specs=[vmem, vmem, vmem],
        out_specs=(vmem, vmem, vmem),
    )(div, eg, qg)
    return div.reshape(GROUP), eg, qg


def solution(mesh):
    in_specs = (
        P("query"),
        P("query"),
        P("query"),
        P(("entity", "query"), None),
        P(("entity", "query"), None),
        P(),
        P(),
    )
    out_specs = (P("query"), P(("entity", "query"), None), P("query", None))
    return jax.shard_map(
        per_device, mesh=mesh, in_specs=in_specs, out_specs=out_specs, check_vma=False
    )
```

```python
import jax
import jax.numpy as jnp
from jax import lax
from jax.experimental import pallas as pl
from jax.experimental.pallas import tpu as pltpu
from jax.sharding import PartitionSpec as P

MESH = pl.DeviceIdType.MESH
BF = jnp.bfloat16
F32 = jnp.float32
GROUP = 512
ROWS = 2 * GROUP
ENT = 128
HALF = 500
PAD = 512
BLK = ENT + 2 * PAD
CUT = BLK // 2
REL = 4131
RELA = 4096
SHARD = 64
BIT = 32


def slot(sd, fd):
    return sd * 4 + fd


def dot_nn(a, b):
    return lax.dot_general(a, b, (((1,), (0,)), ((), ())), preferred_element_type=F32)


def dot_nt(a, b):
    return lax.dot_general(a, b, (((1,), (1,)), ((), ())), preferred_element_type=F32)


def kernel(
    anchors,
    relation_ids,
    flags,
    ent_t,
    ent_s,
    rel_t,
    rel_s,
    div_out,
    eg_out,
    qg_out,
    slab,
    rtv,
    rsv,
    wide,
    mids,
    mrow,
    mcol,
    idb,
    abuf,
    dbuf,
    sumb,
    rbuf,
    racc,
    rsacc,
    qbuf,
    tbuf,
    sbuf,
    mxt,
    mxs,
    zt_acc,
    w_acc,
    zs_acc,
    own_st,
    mate_st,
    st,
    fin,
    ftb,
    fsb,
    qst,
    gbuf,
    eg_own,
    eg_s,
    eg_sr,
    eg_f,
    eg_fr,
    qg,
    qgb,
    qgd,
    qgsum,
    qgz,
    qgr,
    qgo,
    idv,
    ent_v,
    ens_v,
    loc_sem,
    send_sem,
    recv_sem,
):
    q = lax.axis_index("query")
    e = lax.axis_index("entity")
    x, zh, y = lax.div(q, 8), lax.rem(lax.div(q, 4), 2), lax.rem(q, 4)
    zl, core = lax.div(e, 2), lax.rem(e, 2)
    z = zh * 4 + zl
    first = x + core * (y - x)
    second = y + core * (x - y)

    def dev(fd, sd):
        a, b = lax.rem(first + fd, 4), lax.rem(second + sd, 4)
        return (a + core * (b - a)) * 8 + zh * 4 + b + core * (a - b)

    def zdev(d):
        zz = lax.rem(z + d, 8)
        return (x * 8 + lax.div(zz, 4) * 4 + y, lax.rem(zz, 4) * 2 + core)

    mate = (q, zl * 2 + 1 - core)

    moves = ((ent_t, ent_v), (ent_s, ens_v), (anchors, idv.at[0]), (relation_ids, idv.at[1]), (flags, idv.at[2]))
    moves = [pltpu.make_async_copy(a, b, loc_sem.at[2 + i]) for i, (a, b) in enumerate(moves)]
    for move in moves:
        move.start()

    barrier = pltpu.get_barrier_semaphore()
    peers = [(dev(d, 0), e) for d in (1, 2, 3)]
    peers += [(dev(0, d), e) for d in (1, 2, 3)]
    peers += [zdev(d) for d in range(1, 8)]
    peers += [mate]
    for peer in peers:
        pl.semaphore_signal(barrier, inc=1, device_id=peer, device_id_type=MESH)

    rt_copy = pltpu.make_async_copy(rel_t, rtv, loc_sem.at[0])
    rs_copy = pltpu.make_async_copy(rel_s, rsv, loc_sem.at[1])
    for move in moves:
        move.wait()

    slab[0, 0:ENT, :] = ens_v[...]
    wide[0 : 2 * HALF, :] = ent_v[...].astype(F32)
    wide[2 * HALF : 2 * PAD, :] = jnp.zeros((2 * PAD - 2 * HALF, ENT), F32)
    row = lax.broadcasted_iota(jnp.int32, (PAD, ENT), 0)
    slab[0, ENT : ENT + PAD, :] = jnp.where(row < HALF, wide[0:PAD, :], 0.0).astype(BF)
    slab[0, ENT + PAD : BLK, :] = pltpu.roll(wide[...], 2 * PAD - HALF, 0)[0:PAD].astype(BF)
    mids[zh] = jnp.zeros((8, GROUP), jnp.int32)
    for i in range(3):
        mids[zh, i : i + 1, :] = idv[i]
    rt_copy.start()
    rs_copy.start()
    pl.semaphore_wait(barrier, len(peers))

    sent = []
    numbers = {}

    def ship(key, src, dst, target):
        n = len(sent)
        numbers[key] = n
        copy = pltpu.make_async_remote_copy(
            src_ref=src,
            dst_ref=dst,
            send_sem=send_sem.at[n],
            recv_sem=recv_sem.at[n],
            device_id=target,
            device_id_type=MESH,
        )
        copy.start()
        sent.append(copy)

    def await_at(key, dst):
        n = numbers[key]
        pltpu.make_async_remote_copy(
            src_ref=dst,
            dst_ref=dst,
            send_sem=send_sem.at[n],
            recv_sem=recv_sem.at[n],
            device_id=mate,
            device_id_type=MESH,
        ).wait_recv()

    def block(k, half):
        return slab.at[k, pl.ds(half * CUT, CUT), :]

    def push(src, dst, target, half):
        ship(("slab", dst, half), block(src, half), block(dst, half), (target, e))

    def got(k, half):
        await_at(("slab", k, half), block(k, half))

    def f_start():
        for up, down in ((0, 1), (1, 0)):
            push(slot(0, 0), slot(0, 3), dev(1, 0), up)
            push(slot(0, 0), slot(0, 1), dev(3, 0), down)

    def s_start(fd, half):
        for sd in (1, 3) if half == 0 else (3, 1):
            push(slot(0, fd), slot(4 - sd, fd), dev(0, sd), half)

    def f_turn():
        got(slot(0, 3), 0)
        push(slot(0, 3), slot(0, 2), dev(1, 0), 0)
        got(slot(0, 1), 1)
        push(slot(0, 1), slot(0, 2), dev(3, 0), 1)
        s_start(3, 0)
        s_start(1, 1)
        got(slot(0, 3), 1)
        s_start(3, 1)
        got(slot(0, 1), 0)
        s_start(1, 0)

    def f_last():
        for half in range(2):
            got(slot(0, 2), half)
            s_start(2, half)

    def s_turn(fd):
        got(slot(3, fd), 0)
        push(slot(3, fd), slot(2, fd), dev(0, 1), 0)
        got(slot(1, fd), 1)
        push(slot(1, fd), slot(2, fd), dev(0, 3), 1)

    def s_rest():
        for fd in (0, 3, 1, 2):
            got(slot(3, fd), 1)
            got(slot(1, fd), 0)

    lane = lax.broadcasted_iota(jnp.int32, (ROWS, ENT), 1)

    def one_hot(ids, at):
        return jnp.where(ids - at == lane[: ids.shape[0]], 1.0, 0.0).astype(BF)

    def pick(sd, new=False, fds=(0, 1, 2, 3)):
        ks = [slot(sd, fd) for fd in fds]
        hot = jnp.concatenate(
            [one_hot(idb[...], e * 4096 + dev(fd, sd) * ENT) for fd in fds], axis=1
        )
        value = dot_nn(hot, jnp.concatenate([slab[k, 0:ENT, :] for k in ks], axis=0))
        tbuf[4, :, 0:ENT] = value if new else tbuf[4, :, 0:ENT] + value
        for h in range(4):
            lo = ENT + h * 256
            right = jnp.concatenate([slab[k, lo : lo + 256, :] for k in ks], axis=1)
            value = dot_nt(hot, right)
            tbuf[h] = value if new else tbuf[h] + value

    mine = pl.multiple_of(core * GROUP + z * SHARD, SHARD)

    def relations():
        ids = jnp.broadcast_to(mcol[pl.ds(mine, SHARD), 1:2], (SHARD, ENT)).astype(jnp.int32)
        left = REL - RELA
        hot = one_hot(ids, RELA)[:, 0:left]
        racc[...] = jnp.zeros_like(racc)
        racc[:, 0 : 2 * HALF] = dot_nt(hot, rtv[:, RELA:REL])
        rsacc[...] = dot_nn(hot, rsv[RELA:REL, :])

        @pl.loop(0, RELA // 512)
        def _(c):
            at = pl.multiple_of(c * 512, 512)
            hots = jnp.concatenate([one_hot(ids, at + j * ENT) for j in range(4)], axis=1)
            racc[:, 0 : 2 * HALF] += dot_nt(hots, rtv[:, pl.ds(at, 512)])
            rsacc[...] += dot_nn(hots, rsv[pl.ds(at, 512), :])

    f_start()
    s_start(0, 0)
    s_start(0, 1)
    ship("ids", mids.at[zh], mids.at[zh], zdev(4))
    f_turn()
    s_turn(0)
    await_at("ids", mids.at[1 - zh])
    mrow[...] = jnp.zeros_like(mrow)
    for g in range(2):
        mrow[0:8, :] = mids[g].astype(F32)
        flat = jnp.transpose(mrow[...])
        mcol[g * GROUP : (g + 1) * GROUP, :] = flat
        wanted = jnp.broadcast_to(flat[:, 0:1], (GROUP, ENT)).astype(jnp.int32)
        idb[g * GROUP : (g + 1) * GROUP, :] = wanted
    f_last()
    s_turn(3)
    s_turn(1)
    rt_copy.wait()
    rs_copy.wait()
    pick(0, True)
    s_turn(2)
    relations()
    s_rest()
    pick(3)
    pick(1)
    for fds in ((0, 3), (1, 2)):
        for fd in fds:
            got(slot(2, fd), 0)
            got(slot(2, fd), 1)
        pick(2, fds=fds)

    def shard(d, c=None):
        at = lax.rem(z + d, 8) * SHARD
        return pl.ds(pl.multiple_of(at if c is None else c * GROUP + at, SHARD), SHARD)

    order = (4, 3, 5, 2, 6, 1, 7, 0)
    for d in order:
        theirs = shard(d, 1 - core)
        abuf[shard(d), 0:ENT] = tbuf[4, theirs, 0:ENT].astype(BF)
        for h in range(4):
            abuf[shard(d), ENT + h * 256 : ENT + (h + 1) * 256] = tbuf[h, theirs, :].astype(BF)
        ship(("pair", d), abuf.at[shard(d), :], dbuf.at[shard(d), :], mate)

    def merge_cores(d):
        await_at(("pair", d), dbuf.at[shard(d), :])
        came = dbuf[shard(d), :].astype(F32)
        ours = shard(d, core)
        sumb[shard(d), 0:ENT] = (tbuf[4, ours, 0:ENT] + came[:, 0:ENT]).astype(BF)
        for h in range(4):
            cols = slice(ENT + h * 256, ENT + (h + 1) * 256)
            sumb[shard(d), cols] = (tbuf[h, ours, :] + came[:, cols]).astype(BF)

    def part(d, half):
        return pl.ds(pl.multiple_of(lax.rem(z + d, 8) * SHARD + half * BIT, BIT), BIT)

    def chain(way, role):
        return role if way == 0 else 1 - role

    def ring_send(way, role, j):
        d = j if way == 0 else 8 - j
        rows = part(d, chain(way, role))
        at = way * 7 + role * 4 + (4 - role) - j
        ship(("ring", way, role, j), sumb.at[rows, :], rbuf.at[at], zdev(1 if way == 0 else 7))

    def ring_wait(way, role, j):
        at = way * 7 + role * 4 + (4 - role) - j
        await_at(("ring", way, role, j), rbuf.at[at])
        return rbuf[at].astype(F32)

    merge_cores(4)
    for way in range(2):
        ring_send(way, 0, 4)
    for d in order[1:]:
        merge_cores(d)
    for way in range(2):
        ring_send(way, 1, 3)
    for role, j in ((0, 4), (1, 3), (0, 3), (1, 2), (0, 2)):
        for way in range(2):
            came = ring_wait(way, role, j)
            d = j - 1 if way == 0 else 9 - j
            rows = part(d, chain(way, role))
            sumb[rows, :] = (sumb[rows, :].astype(F32) + came).astype(BF)
            ring_send(way, role, j - 1)
    halves = [sumb[part(0, h), :].astype(F32) for h in range(2)]
    for role in (1, 0):
        for way in range(2):
            h = chain(way, role)
            halves[h] = halves[h] + ring_wait(way, role, 1)
    anchor = jnp.concatenate(halves, axis=0)

    sign = 2.0 * mcol[pl.ds(mine, SHARD), 2:3] - 1.0
    a_s, r_s = anchor[:, 0:ENT], rsacc[...]
    a_w, r_w = pltpu.roll(a_s, 64, 1), pltpu.roll(r_s, 64, 1)
    low = lane[:SHARD] < 64
    q_s = jnp.where(low, a_s * r_s - sign * a_w * r_w, a_s * r_w + sign * a_w * r_s)
    a_re, a_im = anchor[:, ENT : ENT + PAD], anchor[:, ENT + PAD : BLK]
    whole = racc[...]
    r_re, r_im = whole[:, 0:PAD], pltpu.roll(whole, 2 * PAD - HALF, 1)[:, 0:PAD]
    qbuf[pl.ds(mine, SHARD), 0:ENT] = q_s.astype(BF)
    qbuf[pl.ds(mine, SHARD), ENT : ENT + PAD] = (a_re * r_re - sign * a_im * r_im).astype(BF)
    qbuf[pl.ds(mine, SHARD), ENT + PAD : BLK] = (a_im * r_re + sign * a_re * r_im).astype(BF)

    def bit(d, half, other=False):
        c = 1 - core if other else core
        at = c * GROUP + lax.rem(z + d, 8) * SHARD + half * BIT
        return qbuf.at[pl.ds(pl.multiple_of(at, BIT), BIT), :]

    def ring_pass(way, role, j):
        d = 8 - (j - 1) if way == 0 else j - 1
        here = bit(d, chain(way, role))
        ship(("pass", way, role, j), here, here, zdev(1 if way == 0 else 7))

    for role in range(2):
        for way in range(2):
            ring_pass(way, role, 1)
    for h in range(2):
        ship(("mate", 0, h), bit(0, h), bit(0, h), mate)

    def pass_on(role, j):
        for way in range(2):
            h = chain(way, role)
            d = 8 - j if way == 0 else j
            await_at(("pass", way, role, j), bit(d, h))
            if j < 3:
                ring_pass(way, role, j + 1)
            if (role, j) == (0, 2):
                ship(("pass", way, 0, 4), bit(d, h), bit(d, h), zdev(2 if way == 0 else 6))
            ship(("mate", d, h), bit(d, h), bit(d, h), mate)

    def score(start, stride, number):
        ds = [(start + stride * i) % 8 for i in range(number)]
        for d in ds:
            for h in range(2):
                await_at(("mate", d, h), bit(d, h, True))

        def rows_at(g, d):
            return pl.ds(pl.multiple_of(g * GROUP + lax.rem(z + d, 8) * SHARD, SHARD), SHARD)

        pieces = [rows_at(g, d) for g in range(2) for d in ds]
        for rows in pieces:
            mxt[rows, :] = jnp.full((SHARD, ENT), -jnp.inf)
            mxs[rows, :] = jnp.full((SHARD, ENT), -jnp.inf)

        @pl.loop(0, 8)
        def _(p):
            k = 2 * p
            left = jnp.concatenate([qbuf[rows, :] for rows in pieces], axis=0)
            right = jnp.concatenate([slab[k, ENT:BLK, :], slab[k + 1, ENT:BLK, :]], axis=1)
            t = dot_nn(left[:, ENT:BLK], right)
            right = jnp.concatenate([slab[k, 0:ENT, :], slab[k + 1, 0:ENT, :]], axis=0)
            s = dot_nt(left[:, 0:ENT], right)
            for i, rows in enumerate(pieces):
                ti, si = t[i * SHARD : (i + 1) * SHARD], s[i * SHARD : (i + 1) * SHARD]
                tbuf[p, rows, :] = ti
                sbuf[p, rows, :] = si
                mxt[rows, :] = jnp.maximum(mxt[rows, :], jnp.maximum(ti[:, 0:ENT], ti[:, ENT:]))
                mxs[rows, :] = jnp.maximum(mxs[rows, :], jnp.maximum(si[:, 0:ENT], si[:, ENT:]))

        @pl.loop(0, 2 * number)
        def _(r):
            g = lax.div(r, number)
            rows = rows_at(g, start + stride * (r - g * number))
            top_t = jnp.broadcast_to(jnp.max(mxt[rows, :], axis=1, keepdims=True), (SHARD, ENT))
            top_s = jnp.broadcast_to(jnp.max(mxs[rows, :], axis=1, keepdims=True), (SHARD, ENT))
            mxt[rows, :] = top_t
            mxs[rows, :] = top_s

            def step(p, carry):
                zt, w, zs = carry
                for h in range(2):
                    cols = slice(h * ENT, (h + 1) * ENT)
                    t, s = tbuf[p, rows, cols], sbuf[p, rows, cols]
                    et, es = jnp.exp(t - top_t), jnp.exp(s - top_s)
                    zt, w, zs = zt + et, w + et * (t - s), zs + es
                    tbuf[p, rows, cols] = et
                    sbuf[p, rows, cols] = es
                return zt, w, zs

            zero = jnp.zeros((SHARD, ENT), F32)
            zt, w, zs = lax.fori_loop(0, 8, step, (zero, zero, zero), unroll=True)
            zt_acc[rows, :] = zt
            w_acc[rows, :] = w
            zs_acc[rows, :] = zs

    score(0, 1, 1)
    pass_on(0, 1)
    pass_on(1, 1)
    score(1, 6, 2)
    pass_on(0, 2)
    pass_on(1, 2)
    score(2, 4, 2)
    for role, j in ((0, 3), (1, 3), (0, 4)):
        pass_on(role, j)
    score(3, 1, 3)

    table = jnp.where(lane == 0, mxt[...], 0.0)
    table = jnp.where(lane == 1, jnp.sum(zt_acc[...], axis=1, keepdims=True), table)
    table = jnp.where(lane == 2, jnp.sum(w_acc[...], axis=1, keepdims=True), table)
    table = jnp.where(lane == 3, mxs[...], table)
    table = jnp.where(lane == 4, jnp.sum(zs_acc[...], axis=1, keepdims=True), table)
    flat = jnp.transpose(table)[0:8, :]
    own_st[0] = flat[:, 0:GROUP]
    own_st[1] = flat[:, GROUP:ROWS]
    ship("pair stats", own_st.at[1 - core], mate_st, mate)
    qst[...] = jnp.transpose(qbuf[:, 0:ENT].astype(F32)).astype(BF)
    await_at("pair stats", mate_st)

    def merge(tables):
        top_t, top_s = tables[0][0:1, :], tables[0][3:4, :]
        for v in tables[1:]:
            top_t, top_s = jnp.maximum(top_t, v[0:1, :]), jnp.maximum(top_s, v[3:4, :])
        total_t = weighted = total_s = jnp.zeros((1, GROUP), F32)
        for v in tables:
            scale_t, scale_s = jnp.exp(v[0:1, :] - top_t), jnp.exp(v[3:4, :] - top_s)
            total_t = total_t + v[1:2, :] * scale_t
            weighted = weighted + v[2:3, :] * scale_t
            total_s = total_s + v[4:5, :] * scale_s
        return top_t, total_t, weighted, top_s, total_s

    st[z] = jnp.zeros((8, GROUP), F32)
    for i, v in enumerate(merge([own_st[core], mate_st[...]])):
        st[z, i : i + 1, :] = v
    for d in range(1, 8):
        ship(("stats", d), st.at[z], st.at[z], zdev(d))
    for d in range(1, 8):
        await_at(("stats", d), st.at[lax.rem(z + 8 - d, 8)])
    top_t, total_t, weighted, top_s, total_s = merge([st[i] for i in range(8)])
    divergence = weighted / total_t - top_t - jnp.log(total_t) + top_s + jnp.log(total_s)
    fin[core] = jnp.zeros((8, GROUP), F32)
    for i, v in enumerate((top_t, total_t, divergence, top_s, total_s)):
        fin[core, i : i + 1, :] = v
    ship("final", fin.at[core], fin.at[core], mate)
    await_at("final", fin.at[1 - core])
    div_out[...] = fin[zh, 2:3, :]
    rowi = lax.broadcasted_iota(jnp.int32, (ENT, GROUP), 0)
    for g in range(2):
        f_t = jnp.exp(own_st[g, 0:1, :] - fin[g, 0:1, :]) / fin[g, 1:2, :]
        f_s = jnp.exp(own_st[g, 3:4, :] - fin[g, 3:4, :]) / fin[g, 4:5, :]
        flipped = jnp.transpose(jnp.where(rowi == 0, f_t, jnp.where(rowi == 1, f_s, 0.0)))
        ftb[g * GROUP : (g + 1) * GROUP, :] = jnp.broadcast_to(flipped[:, 0:1], (GROUP, ENT))
        fsb[g * GROUP : (g + 1) * GROUP, :] = jnp.broadcast_to(flipped[:, 1:2], (GROUP, ENT))

    qg[...] = jnp.zeros_like(qg)

    @pl.loop(0, 8)
    def _(p):
        halves = []
        for h in range(2):
            cols = slice(h * ENT, (h + 1) * ENT)
            g = sbuf[p, :, cols] * fsb[...] - tbuf[p, :, cols] * ftb[...]
            halves.append(g.astype(BF))
        g = jnp.concatenate(halves, axis=1)
        gbuf[p] = g
        right = jnp.concatenate([slab[2 * p, 0:ENT, :], slab[2 * p + 1, 0:ENT, :]], axis=0)
        qg[...] += dot_nn(g, right)

    other = pl.multiple_of((1 - core) * GROUP, GROUP)
    kept = pl.multiple_of(core * GROUP, GROUP)
    qgb[...] = qg[pl.ds(other, GROUP), :].astype(BF)
    ship("pair grad", qgb, qgd, mate)

    def entities(sd):
        @pl.loop(0, 2)
        def _(i):
            grad = dot_nn(qst[...], gbuf[sd * 2 + i])
            for h in range(2):
                cols = slice(h * ENT, (h + 1) * ENT)
                if sd:
                    eg_s[sd - 1, 2 * i + h] = grad[:, cols].astype(BF)
                else:
                    eg_own[2 * i + h] = grad[:, cols]

        if sd:
            ship(("second", sd), eg_s.at[sd - 1], eg_sr.at[sd - 1], (dev(0, sd), e))

    entities(2)
    entities(1)
    await_at("pair grad", qgd)
    qgsum[...] = qg[pl.ds(kept, GROUP), :] + qgd[...].astype(F32)
    qgz[...] = qgsum[...].astype(BF)
    for d in range(1, 8):
        at = pl.multiple_of(lax.rem(z + d, 8) * SHARD, SHARD)
        ship(("shard", d), qgz.at[pl.ds(at, SHARD), :], qgr.at[d - 1], zdev(d))
    entities(3)
    entities(0)
    for sd in (1, 3, 2):
        await_at(("second", sd), eg_sr.at[sd - 1])
    for fd in (2, 1, 3, 0):
        v = eg_own[fd]
        for sd in (1, 2, 3):
            v = v + eg_sr[sd - 1, fd].astype(F32)
        if fd:
            eg_f[fd - 1] = v.astype(BF)
            ship(("first", fd), eg_f.at[fd - 1], eg_fr.at[fd - 1], (dev(fd, 0), e))
        else:
            near = v
    total = qgsum[pl.ds(pl.multiple_of(z * SHARD, SHARD), SHARD), :]
    for d in range(1, 8):
        await_at(("shard", d), qgr.at[d - 1])
    for d in range(1, 8):
        total = total + qgr[d - 1].astype(F32)

    def out_rows(d):
        return qgo.at[core, pl.ds(pl.multiple_of(lax.rem(z + d, 8) * SHARD, SHARD), SHARD), :]

    qgo[core, pl.ds(pl.multiple_of(z * SHARD, SHARD), SHARD), :] = total.astype(BF)
    for d in range(1, 8):
        ship(("sum", d), out_rows(0), out_rows(0), zdev(d))
    for fd in (1, 3, 2):
        await_at(("first", fd), eg_fr.at[fd - 1])
    for fd in (1, 2, 3):
        near = near + eg_fr[fd - 1].astype(F32)
    eg_out[...] = jnp.transpose(near)
    for d in range(1, 8):
        await_at(("sum", d), out_rows(8 - d))
    ship("pair sum", qgo.at[core], qgo.at[core], mate)
    await_at("pair sum", qgo.at[1 - core])
    qg_out[...] = qgo[zh].astype(F32)

    for copy in sent:
        copy.wait_send()


def finish(div, eg, qg, div_out, eg_out, qg_out):
    div_out[...] = div[...]
    eg_out[...] = eg[...]
    qg_out[...] = qg[...]


def per_device(
    anchor_ids,
    relation_ids,
    side_flags,
    teacher_entities,
    student_entities,
    teacher_relations,
    student_relations,
):
    rows = [v.reshape(1, GROUP) for v in (anchor_ids, relation_ids, side_flags)]
    vmem = pl.BlockSpec(memory_space=pltpu.VMEM)
    hbm = pl.BlockSpec(memory_space=pl.ANY)
    big = (ROWS, ENT)
    div, eg, qg = pl.pallas_call(
        kernel,
        out_shape=(
            jax.ShapeDtypeStruct((1, GROUP), F32),
            jax.ShapeDtypeStruct((ENT, ENT), F32),
            jax.ShapeDtypeStruct((GROUP, ENT), F32),
        ),
        in_specs=[hbm] * 7,
        out_specs=(vmem, vmem, vmem),
        scratch_shapes=[
            pltpu.VMEM((16, BLK, ENT), BF),
            pltpu.VMEM((2 * HALF, REL), BF),
            pltpu.VMEM((REL, ENT), BF),
            pltpu.VMEM((2 * PAD, ENT), F32),
            pltpu.VMEM((2, 8, GROUP), jnp.int32),
            pltpu.VMEM((ENT, GROUP), F32),
            pltpu.VMEM(big, F32),
            pltpu.VMEM(big, jnp.int32),
            pltpu.VMEM((GROUP, BLK), BF),
            pltpu.VMEM((GROUP, BLK), BF),
            pltpu.VMEM((GROUP, BLK), BF),
            pltpu.VMEM((14, BIT, BLK), BF),
            pltpu.VMEM((SHARD, 2 * PAD), F32),
            pltpu.VMEM((SHARD, ENT), F32),
            pltpu.VMEM((ROWS, BLK), BF),
            pltpu.VMEM((8, ROWS, 256), F32),
            pltpu.VMEM((8, ROWS, 256), F32),
            pltpu.VMEM(big, F32),
            pltpu.VMEM(big, F32),
            pltpu.VMEM(big, F32),
            pltpu.VMEM(big, F32),
            pltpu.VMEM(big, F32),
            pltpu.VMEM((2, 8, GROUP), F32),
            pltpu.VMEM((8, GROUP), F32),
            pltpu.VMEM((8, 8, GROUP), F32),
            pltpu.VMEM((2, 8, GROUP), F32),
            pltpu.VMEM(big, F32),
            pltpu.VMEM(big, F32),
            pltpu.VMEM((ENT, ROWS), BF),
            pltpu.VMEM((8, ROWS, 256), BF),
            pltpu.VMEM((4, ENT, ENT), F32),
            pltpu.VMEM((3, 4, ENT, ENT), BF),
            pltpu.VMEM((3, 4, ENT, ENT), BF),
            pltpu.VMEM((3, ENT, ENT), BF),
            pltpu.VMEM((3, ENT, ENT), BF),
            pltpu.VMEM(big, F32),
            pltpu.VMEM((GROUP, ENT), BF),
            pltpu.VMEM((GROUP, ENT), BF),
            pltpu.VMEM((GROUP, ENT), F32),
            pltpu.VMEM((GROUP, ENT), BF),
            pltpu.VMEM((7, SHARD, ENT), BF),
            pltpu.VMEM((2, GROUP, ENT), BF),
            pltpu.VMEM((3, 1, GROUP), jnp.int32),
            pltpu.VMEM((2 * HALF, ENT), BF),
            pltpu.VMEM((ENT, ENT), BF),
            pltpu.SemaphoreType.DMA((7,)),
            pltpu.SemaphoreType.DMA((120,)),
            pltpu.SemaphoreType.DMA((120,)),
        ],
        compiler_params=pltpu.CompilerParams(
            collective_id=0, has_side_effects=True, vmem_limit_bytes=60 * 2**20
        ),
    )(*rows, teacher_entities.T, student_entities, teacher_relations.T, student_relations)
    div, eg, qg = pl.pallas_call(
        finish,
        out_shape=(
            jax.ShapeDtypeStruct((1, GROUP), F32),
            jax.ShapeDtypeStruct((ENT, ENT), F32),
            jax.ShapeDtypeStruct((GROUP, ENT), F32),
        ),
        in_specs=[vmem, vmem, vmem],
        out_specs=(vmem, vmem, vmem),
    )(div, eg, qg)
    return div.reshape(GROUP), eg, qg


def solution(mesh):
    in_specs = (
        P("query"),
        P("query"),
        P("query"),
        P(("entity", "query"), None),
        P(("entity", "query"), None),
        P(),
        P(),
    )
    out_specs = (P("query"), P(("entity", "query"), None), P("query", None))
    return jax.shard_map(
        per_device, mesh=mesh, in_specs=in_specs, out_specs=out_specs, check_vma=False
    )
```

```python
import jax
import jax.numpy as jnp
from jax import lax
from jax.experimental import pallas as pl
from jax.experimental.pallas import tpu as pltpu
from jax.sharding import PartitionSpec as P

MESH = pl.DeviceIdType.MESH
BF = jnp.bfloat16
F32 = jnp.float32
GROUP = 512
ROWS = 2 * GROUP
ENT = 128
HALF = 500
PAD = 512
BLK = ENT + 2 * PAD
CUT = BLK // 2
REL = 4131
RELA = 4096
SHARD = 64
BIT = 32


def slot(sd, fd):
    return sd * 4 + fd


def dot_nn(a, b):
    return lax.dot_general(a, b, (((1,), (0,)), ((), ())), preferred_element_type=F32)


def dot_nt(a, b):
    return lax.dot_general(a, b, (((1,), (1,)), ((), ())), preferred_element_type=F32)


def kernel(
    anchors,
    relation_ids,
    flags,
    ent_t,
    ent_s,
    rel_t,
    rel_s,
    div_out,
    eg_out,
    qg_out,
    slab,
    rtv,
    rsv,
    wide,
    mids,
    mrow,
    mcol,
    idb,
    abuf,
    dbuf,
    sumb,
    rbuf,
    racc,
    rsacc,
    qbuf,
    tbuf,
    sbuf,
    mxt,
    mxs,
    zt_acc,
    w_acc,
    zs_acc,
    own_st,
    mate_st,
    st,
    fin,
    ftb,
    fsb,
    qst,
    gbuf,
    eg_own,
    eg_s,
    eg_sr,
    eg_f,
    eg_fr,
    qg,
    qgb,
    qgd,
    qgsum,
    qgz,
    qgr,
    qgo,
    idv,
    ent_v,
    ens_v,
    loc_sem,
    send_sem,
    recv_sem,
):
    q = lax.axis_index("query")
    e = lax.axis_index("entity")
    x, zh, y = lax.div(q, 8), lax.rem(lax.div(q, 4), 2), lax.rem(q, 4)
    zl, core = lax.div(e, 2), lax.rem(e, 2)
    z = zh * 4 + zl
    first = x + core * (y - x)
    second = y + core * (x - y)

    def dev(fd, sd):
        a, b = lax.rem(first + fd, 4), lax.rem(second + sd, 4)
        return (a + core * (b - a)) * 8 + zh * 4 + b + core * (a - b)

    def zdev(d):
        zz = lax.rem(z + d, 8)
        return (x * 8 + lax.div(zz, 4) * 4 + y, lax.rem(zz, 4) * 2 + core)

    mate = (q, zl * 2 + 1 - core)

    moves = ((ent_t, ent_v), (ent_s, ens_v), (anchors, idv.at[0]), (relation_ids, idv.at[1]), (flags, idv.at[2]))
    moves = [pltpu.make_async_copy(a, b, loc_sem.at[2 + i]) for i, (a, b) in enumerate(moves)]
    for move in moves:
        move.start()

    barrier = pltpu.get_barrier_semaphore()
    peers = [(dev(d, 0), e) for d in (1, 2, 3)]
    peers += [(dev(0, d), e) for d in (1, 2, 3)]
    peers += [zdev(d) for d in range(1, 8)]
    peers += [mate]
    for peer in peers:
        pl.semaphore_signal(barrier, inc=1, device_id=peer, device_id_type=MESH)

    rt_copy = pltpu.make_async_copy(rel_t, rtv, loc_sem.at[0])
    rs_copy = pltpu.make_async_copy(rel_s, rsv, loc_sem.at[1])
    for move in moves:
        move.wait()

    slab[0, 0:ENT, :] = ens_v[...]
    wide[0 : 2 * HALF, :] = ent_v[...].astype(F32)
    wide[2 * HALF : 2 * PAD, :] = jnp.zeros((2 * PAD - 2 * HALF, ENT), F32)
    row = lax.broadcasted_iota(jnp.int32, (PAD, ENT), 0)
    slab[0, ENT : ENT + PAD, :] = jnp.where(row < HALF, wide[0:PAD, :], 0.0).astype(BF)
    slab[0, ENT + PAD : BLK, :] = pltpu.roll(wide[...], 2 * PAD - HALF, 0)[0:PAD].astype(BF)
    mids[zh] = jnp.zeros((8, GROUP), jnp.int32)
    for i in range(3):
        mids[zh, i : i + 1, :] = idv[i]
    rt_copy.start()
    rs_copy.start()
    pl.semaphore_wait(barrier, len(peers))

    sent = []
    numbers = {}

    def ship(key, src, dst, target):
        n = len(sent)
        numbers[key] = n
        copy = pltpu.make_async_remote_copy(
            src_ref=src,
            dst_ref=dst,
            send_sem=send_sem.at[n],
            recv_sem=recv_sem.at[n],
            device_id=target,
            device_id_type=MESH,
        )
        copy.start()
        sent.append(copy)

    def await_at(key, dst):
        n = numbers[key]
        pltpu.make_async_remote_copy(
            src_ref=dst,
            dst_ref=dst,
            send_sem=send_sem.at[n],
            recv_sem=recv_sem.at[n],
            device_id=mate,
            device_id_type=MESH,
        ).wait_recv()

    def block(k, half):
        return slab.at[k, pl.ds(half * CUT, CUT), :]

    def push(src, dst, target, half):
        ship(("slab", dst, half), block(src, half), block(dst, half), (target, e))

    def got(k, half):
        await_at(("slab", k, half), block(k, half))

    def f_start():
        for up, down in ((0, 1), (1, 0)):
            push(slot(0, 0), slot(0, 3), dev(1, 0), up)
            push(slot(0, 0), slot(0, 1), dev(3, 0), down)

    def s_start(fd, half):
        for sd in (1, 3) if half == 0 else (3, 1):
            push(slot(0, fd), slot(4 - sd, fd), dev(0, sd), half)

    def f_turn():
        got(slot(0, 3), 0)
        push(slot(0, 3), slot(0, 2), dev(1, 0), 0)
        got(slot(0, 1), 1)
        push(slot(0, 1), slot(0, 2), dev(3, 0), 1)
        s_start(3, 0)
        s_start(1, 1)
        got(slot(0, 3), 1)
        s_start(3, 1)
        got(slot(0, 1), 0)
        s_start(1, 0)

    def f_last():
        for half in range(2):
            got(slot(0, 2), half)
            s_start(2, half)

    def s_turn(fd):
        got(slot(3, fd), 0)
        push(slot(3, fd), slot(2, fd), dev(0, 1), 0)
        got(slot(1, fd), 1)
        push(slot(1, fd), slot(2, fd), dev(0, 3), 1)

    def s_rest():
        for fd in (0, 3, 1, 2):
            got(slot(3, fd), 1)
            got(slot(1, fd), 0)

    lane = lax.broadcasted_iota(jnp.int32, (ROWS, ENT), 1)

    def one_hot(ids, at):
        return jnp.where(ids - at == lane[: ids.shape[0]], 1.0, 0.0).astype(BF)

    def pick(sd, new=False, fds=(0, 1, 2, 3)):
        ks = [slot(sd, fd) for fd in fds]
        hot = jnp.concatenate(
            [one_hot(idb[...], e * 4096 + dev(fd, sd) * ENT) for fd in fds], axis=1
        )
        value = dot_nn(hot, jnp.concatenate([slab[k, 0:ENT, :] for k in ks], axis=0))
        tbuf[4, :, 0:ENT] = value if new else tbuf[4, :, 0:ENT] + value
        for h in range(4):
            lo = ENT + h * 256
            right = jnp.concatenate([slab[k, lo : lo + 256, :] for k in ks], axis=1)
            value = dot_nt(hot, right)
            tbuf[h] = value if new else tbuf[h] + value

    mine = pl.multiple_of(core * GROUP + z * SHARD, SHARD)

    def relations():
        ids = jnp.broadcast_to(mcol[pl.ds(mine, SHARD), 1:2], (SHARD, ENT)).astype(jnp.int32)
        left = REL - RELA
        hot = one_hot(ids, RELA)[:, 0:left]
        racc[...] = jnp.zeros_like(racc)
        racc[:, 0 : 2 * HALF] = dot_nt(hot, rtv[:, RELA:REL])
        rsacc[...] = dot_nn(hot, rsv[RELA:REL, :])

        @pl.loop(0, RELA // 512)
        def _(c):
            at = pl.multiple_of(c * 512, 512)
            hots = jnp.concatenate([one_hot(ids, at + j * ENT) for j in range(4)], axis=1)
            racc[:, 0 : 2 * HALF] += dot_nt(hots, rtv[:, pl.ds(at, 512)])
            rsacc[...] += dot_nn(hots, rsv[pl.ds(at, 512), :])

    f_start()
    s_start(0, 0)
    s_start(0, 1)
    ship("ids", mids.at[zh], mids.at[zh], zdev(4))
    f_turn()
    s_turn(0)
    await_at("ids", mids.at[1 - zh])
    mrow[...] = jnp.zeros_like(mrow)
    for g in range(2):
        mrow[0:8, :] = mids[g].astype(F32)
        flat = jnp.transpose(mrow[...])
        mcol[g * GROUP : (g + 1) * GROUP, :] = flat
        wanted = jnp.broadcast_to(flat[:, 0:1], (GROUP, ENT)).astype(jnp.int32)
        idb[g * GROUP : (g + 1) * GROUP, :] = wanted
    f_last()
    s_turn(3)
    s_turn(1)
    rt_copy.wait()
    rs_copy.wait()
    pick(0, True)
    s_turn(2)
    relations()
    s_rest()
    pick(3)
    pick(1)
    for fds in ((0, 3), (1, 2)):
        for fd in fds:
            got(slot(2, fd), 0)
            got(slot(2, fd), 1)
        pick(2, fds=fds)

    def shard(d, c=None):
        at = lax.rem(z + d, 8) * SHARD
        return pl.ds(pl.multiple_of(at if c is None else c * GROUP + at, SHARD), SHARD)

    order = (4, 3, 5, 2, 6, 1, 7, 0)
    for d in order:
        theirs = shard(d, 1 - core)
        abuf[shard(d), 0:ENT] = tbuf[4, theirs, 0:ENT].astype(BF)
        for h in range(4):
            abuf[shard(d), ENT + h * 256 : ENT + (h + 1) * 256] = tbuf[h, theirs, :].astype(BF)
        ship(("pair", d), abuf.at[shard(d), :], dbuf.at[shard(d), :], mate)

    def merge_cores(d):
        await_at(("pair", d), dbuf.at[shard(d), :])
        came = dbuf[shard(d), :].astype(F32)
        ours = shard(d, core)
        sumb[shard(d), 0:ENT] = (tbuf[4, ours, 0:ENT] + came[:, 0:ENT]).astype(BF)
        for h in range(4):
            cols = slice(ENT + h * 256, ENT + (h + 1) * 256)
            sumb[shard(d), cols] = (tbuf[h, ours, :] + came[:, cols]).astype(BF)

    def part(d, half):
        return pl.ds(pl.multiple_of(lax.rem(z + d, 8) * SHARD + half * BIT, BIT), BIT)

    def chain(way, role):
        return role if way == 0 else 1 - role

    def ring_send(way, role, j):
        d = j if way == 0 else 8 - j
        rows = part(d, chain(way, role))
        at = way * 7 + role * 4 + (4 - role) - j
        ship(("ring", way, role, j), sumb.at[rows, :], rbuf.at[at], zdev(1 if way == 0 else 7))

    def ring_wait(way, role, j):
        at = way * 7 + role * 4 + (4 - role) - j
        await_at(("ring", way, role, j), rbuf.at[at])
        return rbuf[at].astype(F32)

    merge_cores(4)
    for way in range(2):
        ring_send(way, 0, 4)
    for d in order[1:]:
        merge_cores(d)
    for way in range(2):
        ring_send(way, 1, 3)
    for role, j in ((0, 4), (1, 3), (0, 3), (1, 2), (0, 2)):
        for way in range(2):
            came = ring_wait(way, role, j)
            d = j - 1 if way == 0 else 9 - j
            rows = part(d, chain(way, role))
            sumb[rows, :] = (sumb[rows, :].astype(F32) + came).astype(BF)
            ring_send(way, role, j - 1)
    halves = [sumb[part(0, h), :].astype(F32) for h in range(2)]
    for role in (1, 0):
        for way in range(2):
            h = chain(way, role)
            halves[h] = halves[h] + ring_wait(way, role, 1)
    anchor = jnp.concatenate(halves, axis=0)

    sign = 2.0 * mcol[pl.ds(mine, SHARD), 2:3] - 1.0
    a_s, r_s = anchor[:, 0:ENT], rsacc[...]
    a_w, r_w = pltpu.roll(a_s, 64, 1), pltpu.roll(r_s, 64, 1)
    low = lane[:SHARD] < 64
    q_s = jnp.where(low, a_s * r_s - sign * a_w * r_w, a_s * r_w + sign * a_w * r_s)
    a_re, a_im = anchor[:, ENT : ENT + PAD], anchor[:, ENT + PAD : BLK]
    whole = racc[...]
    r_re, r_im = whole[:, 0:PAD], pltpu.roll(whole, 2 * PAD - HALF, 1)[:, 0:PAD]
    qbuf[pl.ds(mine, SHARD), 0:ENT] = q_s.astype(BF)
    qbuf[pl.ds(mine, SHARD), ENT : ENT + PAD] = (a_re * r_re - sign * a_im * r_im).astype(BF)
    qbuf[pl.ds(mine, SHARD), ENT + PAD : BLK] = (a_im * r_re + sign * a_re * r_im).astype(BF)

    def bit(d, half, other=False):
        c = 1 - core if other else core
        at = c * GROUP + lax.rem(z + d, 8) * SHARD + half * BIT
        return qbuf.at[pl.ds(pl.multiple_of(at, BIT), BIT), :]

    def ring_pass(way, role, j):
        d = 8 - (j - 1) if way == 0 else j - 1
        here = bit(d, chain(way, role))
        ship(("pass", way, role, j), here, here, zdev(1 if way == 0 else 7))

    for role in range(2):
        for way in range(2):
            ring_pass(way, role, 1)
    for h in range(2):
        ship(("mate", 0, h), bit(0, h), bit(0, h), mate)

    def pass_on(role, j):
        for way in range(2):
            h = chain(way, role)
            d = 8 - j if way == 0 else j
            await_at(("pass", way, role, j), bit(d, h))
            if j < 3:
                ring_pass(way, role, j + 1)
            if (role, j) == (0, 2):
                ship(("pass", way, 0, 4), bit(d, h), bit(d, h), zdev(2 if way == 0 else 6))
            ship(("mate", d, h), bit(d, h), bit(d, h), mate)

    def score(start, stride, number):
        ds = [(start + stride * i) % 8 for i in range(number)]
        for d in ds:
            for h in range(2):
                await_at(("mate", d, h), bit(d, h, True))

        def rows_at(g, d):
            return pl.ds(pl.multiple_of(g * GROUP + lax.rem(z + d, 8) * SHARD, SHARD), SHARD)

        pieces = [rows_at(g, d) for g in range(2) for d in ds]
        for rows in pieces:
            mxt[rows, :] = jnp.full((SHARD, ENT), -jnp.inf)
            mxs[rows, :] = jnp.full((SHARD, ENT), -jnp.inf)

        @pl.loop(0, 8)
        def _(p):
            k = 2 * p
            left = jnp.concatenate([qbuf[rows, :] for rows in pieces], axis=0)
            right = jnp.concatenate([slab[k, ENT:BLK, :], slab[k + 1, ENT:BLK, :]], axis=1)
            t = dot_nn(left[:, ENT:BLK], right)
            right = jnp.concatenate([slab[k, 0:ENT, :], slab[k + 1, 0:ENT, :]], axis=0)
            s = dot_nt(left[:, 0:ENT], right)
            for i, rows in enumerate(pieces):
                ti, si = t[i * SHARD : (i + 1) * SHARD], s[i * SHARD : (i + 1) * SHARD]
                tbuf[p, rows, :] = ti
                sbuf[p, rows, :] = si
                mxt[rows, :] = jnp.maximum(mxt[rows, :], jnp.maximum(ti[:, 0:ENT], ti[:, ENT:]))
                mxs[rows, :] = jnp.maximum(mxs[rows, :], jnp.maximum(si[:, 0:ENT], si[:, ENT:]))

        @pl.loop(0, 2 * number)
        def _(r):
            g = lax.div(r, number)
            rows = rows_at(g, start + stride * (r - g * number))
            top_t = jnp.broadcast_to(jnp.max(mxt[rows, :], axis=1, keepdims=True), (SHARD, ENT))
            top_s = jnp.broadcast_to(jnp.max(mxs[rows, :], axis=1, keepdims=True), (SHARD, ENT))
            mxt[rows, :] = top_t
            mxs[rows, :] = top_s

            def step(p, carry):
                zt, w, zs = carry
                for h in range(2):
                    cols = slice(h * ENT, (h + 1) * ENT)
                    t, s = tbuf[p, rows, cols], sbuf[p, rows, cols]
                    et, es = jnp.exp(t - top_t), jnp.exp(s - top_s)
                    zt, w, zs = zt + et, w + et * (t - s), zs + es
                    tbuf[p, rows, cols] = et
                    sbuf[p, rows, cols] = es
                return zt, w, zs

            zero = jnp.zeros((SHARD, ENT), F32)
            zt, w, zs = lax.fori_loop(0, 8, step, (zero, zero, zero), unroll=True)
            zt_acc[rows, :] = zt
            w_acc[rows, :] = w
            zs_acc[rows, :] = zs

    score(0, 1, 1)
    pass_on(0, 1)
    pass_on(1, 1)
    score(1, 6, 2)
    pass_on(0, 2)
    pass_on(1, 2)
    score(2, 4, 2)
    for role, j in ((0, 3), (1, 3), (0, 4)):
        pass_on(role, j)
    score(3, 1, 3)

    table = jnp.where(lane == 0, mxt[...], 0.0)
    table = jnp.where(lane == 1, jnp.sum(zt_acc[...], axis=1, keepdims=True), table)
    table = jnp.where(lane == 2, jnp.sum(w_acc[...], axis=1, keepdims=True), table)
    table = jnp.where(lane == 3, mxs[...], table)
    table = jnp.where(lane == 4, jnp.sum(zs_acc[...], axis=1, keepdims=True), table)
    flat = jnp.transpose(table)[0:8, :]
    own_st[0] = flat[:, 0:GROUP]
    own_st[1] = flat[:, GROUP:ROWS]
    ship("pair stats", own_st.at[1 - core], mate_st, mate)
    qst[...] = jnp.transpose(qbuf[:, 0:ENT].astype(F32)).astype(BF)
    await_at("pair stats", mate_st)

    def merge(tables):
        top_t, top_s = tables[0][0:1, :], tables[0][3:4, :]
        for v in tables[1:]:
            top_t, top_s = jnp.maximum(top_t, v[0:1, :]), jnp.maximum(top_s, v[3:4, :])
        total_t = weighted = total_s = jnp.zeros((1, GROUP), F32)
        for v in tables:
            scale_t, scale_s = jnp.exp(v[0:1, :] - top_t), jnp.exp(v[3:4, :] - top_s)
            total_t = total_t + v[1:2, :] * scale_t
            weighted = weighted + v[2:3, :] * scale_t
            total_s = total_s + v[4:5, :] * scale_s
        return top_t, total_t, weighted, top_s, total_s

    st[z] = jnp.zeros((8, GROUP), F32)
    for i, v in enumerate(merge([own_st[core], mate_st[...]])):
        st[z, i : i + 1, :] = v
    for d in order[:7]:
        ship(("stats", d), st.at[z], st.at[z], zdev(d))
    for d in range(1, 8):
        await_at(("stats", d), st.at[lax.rem(z + 8 - d, 8)])
    top_t, total_t, weighted, top_s, total_s = merge([st[i] for i in range(8)])
    divergence = weighted / total_t - top_t - jnp.log(total_t) + top_s + jnp.log(total_s)
    fin[core] = jnp.zeros((8, GROUP), F32)
    for i, v in enumerate((top_t, total_t, divergence, top_s, total_s)):
        fin[core, i : i + 1, :] = v
    ship("final", fin.at[core], fin.at[core], mate)
    await_at("final", fin.at[1 - core])
    div_out[...] = fin[zh, 2:3, :]
    rowi = lax.broadcasted_iota(jnp.int32, (ENT, GROUP), 0)
    for g in range(2):
        f_t = jnp.exp(own_st[g, 0:1, :] - fin[g, 0:1, :]) / fin[g, 1:2, :]
        f_s = jnp.exp(own_st[g, 3:4, :] - fin[g, 3:4, :]) / fin[g, 4:5, :]
        flipped = jnp.transpose(jnp.where(rowi == 0, f_t, jnp.where(rowi == 1, f_s, 0.0)))
        ftb[g * GROUP : (g + 1) * GROUP, :] = jnp.broadcast_to(flipped[:, 0:1], (GROUP, ENT))
        fsb[g * GROUP : (g + 1) * GROUP, :] = jnp.broadcast_to(flipped[:, 1:2], (GROUP, ENT))

    qg[...] = jnp.zeros_like(qg)

    other = pl.multiple_of((1 - core) * GROUP, GROUP)
    kept = pl.multiple_of(core * GROUP, GROUP)

    def weights(rows):
        @pl.loop(0, 8)
        def _(p):
            halves = []
            for h in range(2):
                cols = slice(h * ENT, (h + 1) * ENT)
                g = sbuf[p, rows, cols] * fsb[rows, :] - tbuf[p, rows, cols] * ftb[rows, :]
                halves.append(g.astype(BF))
            g = jnp.concatenate(halves, axis=1)
            gbuf[p, rows, :] = g
            right = jnp.concatenate([slab[2 * p, 0:ENT, :], slab[2 * p + 1, 0:ENT, :]], axis=0)
            qg[rows, :] += dot_nn(g, right)

    weights(pl.ds(other, GROUP))
    qgb[...] = qg[pl.ds(other, GROUP), :].astype(BF)
    ship("pair grad", qgb, qgd, mate)
    weights(pl.ds(kept, GROUP))
    await_at("pair grad", qgd)
    qgsum[...] = qg[pl.ds(kept, GROUP), :] + qgd[...].astype(F32)
    qgz[...] = qgsum[...].astype(BF)
    for d in order[:7]:
        at = pl.multiple_of(lax.rem(z + d, 8) * SHARD, SHARD)
        ship(("shard", d), qgz.at[pl.ds(at, SHARD), :], qgr.at[d - 1], zdev(d))

    def entities(sd):
        @pl.loop(0, 2)
        def _(i):
            grad = dot_nn(qst[...], gbuf[sd * 2 + i])
            for h in range(2):
                cols = slice(h * ENT, (h + 1) * ENT)
                if sd:
                    eg_s[sd - 1, 2 * i + h] = grad[:, cols].astype(BF)
                else:
                    eg_own[2 * i + h] = grad[:, cols]

        if sd:
            ship(("second", sd), eg_s.at[sd - 1], eg_sr.at[sd - 1], (dev(0, sd), e))

    entities(2)
    entities(1)
    entities(3)
    entities(0)
    for sd in (1, 3, 2):
        await_at(("second", sd), eg_sr.at[sd - 1])
    for fd in (2, 1, 3, 0):
        v = eg_own[fd]
        for sd in (1, 2, 3):
            v = v + eg_sr[sd - 1, fd].astype(F32)
        if fd:
            eg_f[fd - 1] = v.astype(BF)
            ship(("first", fd), eg_f.at[fd - 1], eg_fr.at[fd - 1], (dev(fd, 0), e))
        else:
            near = v
    total = qgsum[pl.ds(pl.multiple_of(z * SHARD, SHARD), SHARD), :]
    for d in range(1, 8):
        await_at(("shard", d), qgr.at[d - 1])
    for d in range(1, 8):
        total = total + qgr[d - 1].astype(F32)

    def out_rows(d):
        return qgo.at[core, pl.ds(pl.multiple_of(lax.rem(z + d, 8) * SHARD, SHARD), SHARD), :]

    qgo[core, pl.ds(pl.multiple_of(z * SHARD, SHARD), SHARD), :] = total.astype(BF)
    for d in order[:7]:
        ship(("sum", d), out_rows(0), out_rows(0), zdev(d))
    for fd in (1, 3, 2):
        await_at(("first", fd), eg_fr.at[fd - 1])
    for fd in (1, 2, 3):
        near = near + eg_fr[fd - 1].astype(F32)
    eg_out[...] = jnp.transpose(near)
    for d in range(1, 8):
        await_at(("sum", d), out_rows(8 - d))
    ship("pair sum", qgo.at[core], qgo.at[core], mate)
    await_at("pair sum", qgo.at[1 - core])
    qg_out[...] = qgo[zh].astype(F32)

    for copy in sent:
        copy.wait_send()


def finish(div, eg, qg, div_out, eg_out, qg_out):
    div_out[...] = div[...]
    eg_out[...] = eg[...]
    qg_out[...] = qg[...]


def per_device(
    anchor_ids,
    relation_ids,
    side_flags,
    teacher_entities,
    student_entities,
    teacher_relations,
    student_relations,
):
    rows = [v.reshape(1, GROUP) for v in (anchor_ids, relation_ids, side_flags)]
    vmem = pl.BlockSpec(memory_space=pltpu.VMEM)
    hbm = pl.BlockSpec(memory_space=pl.ANY)
    big = (ROWS, ENT)
    div, eg, qg = pl.pallas_call(
        kernel,
        out_shape=(
            jax.ShapeDtypeStruct((1, GROUP), F32),
            jax.ShapeDtypeStruct((ENT, ENT), F32),
            jax.ShapeDtypeStruct((GROUP, ENT), F32),
        ),
        in_specs=[hbm] * 7,
        out_specs=(vmem, vmem, vmem),
        scratch_shapes=[
            pltpu.VMEM((16, BLK, ENT), BF),
            pltpu.VMEM((2 * HALF, REL), BF),
            pltpu.VMEM((REL, ENT), BF),
            pltpu.VMEM((2 * PAD, ENT), F32),
            pltpu.VMEM((2, 8, GROUP), jnp.int32),
            pltpu.VMEM((ENT, GROUP), F32),
            pltpu.VMEM(big, F32),
            pltpu.VMEM(big, jnp.int32),
            pltpu.VMEM((GROUP, BLK), BF),
            pltpu.VMEM((GROUP, BLK), BF),
            pltpu.VMEM((GROUP, BLK), BF),
            pltpu.VMEM((14, BIT, BLK), BF),
            pltpu.VMEM((SHARD, 2 * PAD), F32),
            pltpu.VMEM((SHARD, ENT), F32),
            pltpu.VMEM((ROWS, BLK), BF),
            pltpu.VMEM((8, ROWS, 256), F32),
            pltpu.VMEM((8, ROWS, 256), F32),
            pltpu.VMEM(big, F32),
            pltpu.VMEM(big, F32),
            pltpu.VMEM(big, F32),
            pltpu.VMEM(big, F32),
            pltpu.VMEM(big, F32),
            pltpu.VMEM((2, 8, GROUP), F32),
            pltpu.VMEM((8, GROUP), F32),
            pltpu.VMEM((8, 8, GROUP), F32),
            pltpu.VMEM((2, 8, GROUP), F32),
            pltpu.VMEM(big, F32),
            pltpu.VMEM(big, F32),
            pltpu.VMEM((ENT, ROWS), BF),
            pltpu.VMEM((8, ROWS, 256), BF),
            pltpu.VMEM((4, ENT, ENT), F32),
            pltpu.VMEM((3, 4, ENT, ENT), BF),
            pltpu.VMEM((3, 4, ENT, ENT), BF),
            pltpu.VMEM((3, ENT, ENT), BF),
            pltpu.VMEM((3, ENT, ENT), BF),
            pltpu.VMEM(big, F32),
            pltpu.VMEM((GROUP, ENT), BF),
            pltpu.VMEM((GROUP, ENT), BF),
            pltpu.VMEM((GROUP, ENT), F32),
            pltpu.VMEM((GROUP, ENT), BF),
            pltpu.VMEM((7, SHARD, ENT), BF),
            pltpu.VMEM((2, GROUP, ENT), BF),
            pltpu.VMEM((3, 1, GROUP), jnp.int32),
            pltpu.VMEM((2 * HALF, ENT), BF),
            pltpu.VMEM((ENT, ENT), BF),
            pltpu.SemaphoreType.DMA((7,)),
            pltpu.SemaphoreType.DMA((120,)),
            pltpu.SemaphoreType.DMA((120,)),
        ],
        compiler_params=pltpu.CompilerParams(
            collective_id=0, has_side_effects=True, vmem_limit_bytes=60 * 2**20
        ),
    )(*rows, teacher_entities.T, student_entities, teacher_relations.T, student_relations)
    div, eg, qg = pl.pallas_call(
        finish,
        out_shape=(
            jax.ShapeDtypeStruct((1, GROUP), F32),
            jax.ShapeDtypeStruct((ENT, ENT), F32),
            jax.ShapeDtypeStruct((GROUP, ENT), F32),
        ),
        in_specs=[vmem, vmem, vmem],
        out_specs=(vmem, vmem, vmem),
    )(div, eg, qg)
    return div.reshape(GROUP), eg, qg


def solution(mesh):
    in_specs = (
        P("query"),
        P("query"),
        P("query"),
        P(("entity", "query"), None),
        P(("entity", "query"), None),
        P(),
        P(),
    )
    out_specs = (P("query"), P(("entity", "query"), None), P("query", None))
    return jax.shard_map(
        per_device, mesh=mesh, in_specs=in_specs, out_specs=out_specs, check_vma=False
    )
```
